32 devices in a mesh: dp: 8 (over z, x), mp: 4 (over y, core).
Axes of the slice: x: 2, y: 2, z: 4, core: 2. Of those that a mesh axis runs over, the one named last changes fastest.
Arguments:
- teacher_query: bfloat16 [512, 8192], P('mp', 'dp'), may hold values from -120 to 120
- teacher_keys: bfloat16 [512, 1024], P('mp'), may hold values from -6 to 6
- teacher_values: bfloat16 [512, 1024], P('mp'), may hold values from -6 to 6
- teacher_out: bfloat16 [8192, 8192], P('dp', 'mp'), may hold values from -0.0625 to 0.0625
- teacher_resid: bfloat16 [512, 8192], P('dp', 'mp'), may hold values from -1.5 to 1.5
- distill_proj: bfloat16 [8192, 4096], P('mp', 'dp'), may hold values from -1 to 2
- student_context: bfloat16 [512, 4096], P('mp'), may hold values from -6 to 6
- student_resid: bfloat16 [512, 4096], P('mp', 'dp'), may hold values from -3 to 3
- student_out: bfloat16 [4096, 4096], P(None, 'dp'), may hold values from -0.09375 to 0.09375
- student_gain: float32 [4096], replicated, may hold values from 0.5 to 1.5
Outputs:
- grad_wo: bfloat16 [4096, 4096], P(None, 'dp')
- grad_gain: float32 [4096], P('dp')
- grad_proj: float32 [8192, 4096], P('mp', 'dp')
The draws below stay inside these ranges and needn't reach their ends.
All inputs are finite; a program needn't handle non-finite values.
Results may differ from the reference program's by a relative error of at most 0.03.
Values may be sent and summed in bfloat16 or wider, within the bound.
A program may use at most 64 MiB of HBM per device.

```python
import jax
import jax.numpy as jnp
from jax import lax

D_T = 8192
HEADS = 64
KV_HEADS = 8
HEAD = 128
D_S = 4096
TOKENS = 512
N_DP = 8


def shared_keys(key):
    return jnp.clip(jax.random.normal(key, (TOKENS, KV_HEADS * HEAD), jnp.float32), -6.0, 6.0)


def shared_resid(key):
    source = jax.random.fold_in(key, 101)
    return jnp.clip(0.3 * jax.random.normal(source, (TOKENS, D_T), jnp.float32), -1.5, 1.5)


def draw_teacher_keys(key, part):
    keys = shared_keys(key)
    return keys.astype(jnp.bfloat16)


def draw_teacher_query(key, part):
    key = jax.random.fold_in(key, 23)
    base = jnp.clip(1.5 * jax.random.normal(key, (TOKENS, HEADS * HEAD), jnp.float32), -9.0, 9.0)
    return base.astype(jnp.bfloat16)


def draw_teacher_resid(key, part):
    return shared_resid(key).astype(jnp.bfloat16)


def draw_student_resid(key, part):
    resid = shared_resid(key)
    key = jax.random.fold_in(key, 37)
    noise = jax.random.normal(key, (TOKENS, D_S), jnp.float32)
    values = 3.3 * resid[:, :D_S] + 0.5 * noise
    return jnp.clip(values, -3.0, 3.0).astype(jnp.bfloat16)


def draw_distill_proj(key, part):
    key = jax.random.fold_in(key, 41)
    weights = jnp.clip(jax.random.normal(key, (D_T, D_S), jnp.float32), -6.0, 6.0) * D_T ** (-0.5)
    rows = lax.iota(jnp.int32, D_T)
    cols = lax.iota(jnp.int32, D_S)
    embed = rows[:, None] % D_S == cols[None, :]
    values = weights + jnp.where(embed, 1.5 * (D_S / D_T) ** 0.5, 0.0)
    return values.astype(jnp.bfloat16)


def level_of(rng, extent, shards, smallest, largest):
    gain = 1.0
    for axis_at, shards_of in shards:
        heights = jax.random.uniform(jax.random.fold_in(jax.random.fold_in(rng, 6), axis_at), (shards_of,), jnp.float32, smallest / len(shards), largest / len(shards))
        gain = gain * jnp.repeat(jnp.exp(heights), extent[axis_at] // shards_of).reshape((-1,) + (1,) * (len(extent) - 1 - axis_at))
    return gain


def scatter_about(own_key, dims, deviation, most, pieces=(), held_as=jnp.bfloat16):
    level = level_of(own_key, dims, pieces, -0.22, 0.18) if pieces else 1.0
    drawn = jax.random.normal(own_key, dims, jnp.float32) * deviation * level
    return jnp.minimum(jnp.maximum(drawn, -most), most).astype(held_as)


def setup_inputs(seed: int = 0) -> dict:
    splits = jax.random.split(jax.random.key(seed), 11)
    teacher_query = draw_teacher_query(jax.random.fold_in(splits[10], 71), 0)
    teacher_keys = draw_teacher_keys(jax.random.fold_in(splits[10], 71), 0)
    teacher_values = scatter_about(splits[2], (TOKENS, KV_HEADS * HEAD), 1.0, 6.0, ((0, 4),))
    teacher_out = scatter_about(splits[3], (D_T, D_T), D_T ** -0.5, 0.0625, ((0, 8), (1, 4)))
    teacher_resid = draw_teacher_resid(jax.random.fold_in(splits[10], 71), 0)
    distill_proj = draw_distill_proj(jax.random.fold_in(splits[10], 71), 0)
    student_context = scatter_about(splits[6], (TOKENS, D_S), 1.0, 6.0, ((0, 4),))
    student_resid = draw_student_resid(jax.random.fold_in(splits[10], 71), 0)
    student_out = scatter_about(splits[8], (D_S, D_S), D_S ** -0.5, 0.09375, ((1, 8),))
    student_gain = jnp.clip(1.0 + 0.1 * jax.random.normal(splits[9], (D_S,), jnp.float32), 0.5, 1.5)
    return {"teacher_query": teacher_query, "teacher_keys": teacher_keys, "teacher_values": teacher_values, "teacher_out": teacher_out, "teacher_resid": teacher_resid, "distill_proj": distill_proj, "student_context": student_context, "student_resid": student_resid, "student_out": student_out, "student_gain": student_gain}


EPS = 1e-05

def reference(teacher_query, teacher_keys, teacher_values, teacher_out, teacher_resid, distill_proj, student_context, student_resid, student_out, student_gain):
    groups = HEADS // KV_HEADS
    query_heads = teacher_query.reshape(TOKENS, HEADS, HEAD).transpose(1, 0, 2)
    key_heads = teacher_keys.reshape(TOKENS, KV_HEADS, HEAD).transpose(1, 0, 2)
    value_heads = teacher_values.reshape(TOKENS, KV_HEADS, HEAD).transpose(1, 0, 2)
    positions = lax.iota(jnp.int32, TOKENS)
    allowed = positions[:, None] >= positions[None, :]

    def one_head(index):
        query = lax.dynamic_index_in_dim(query_heads, index, 0, keepdims=False)
        shared = (index // groups).astype(jnp.int32)
        keys = lax.dynamic_index_in_dim(key_heads, shared, 0, keepdims=False)
        values = lax.dynamic_index_in_dim(value_heads, shared, 0, keepdims=False)
        scores = jnp.dot(query, keys.T, preferred_element_type=jnp.float32) * HEAD ** (-0.5)
        scores = jnp.where(allowed, scores, -jnp.inf)
        top = lax.optimization_barrier(jnp.max(scores, axis=1, keepdims=True))
        weights = jnp.exp(scores - top)
        probs = (weights / lax.optimization_barrier(jnp.sum(weights, axis=1, keepdims=True))).astype(jnp.bfloat16)
        return jnp.dot(probs, values, preferred_element_type=jnp.float32).astype(jnp.bfloat16)
    context = lax.map(one_head, jnp.arange(HEADS, dtype=jnp.int32))
    context = context.transpose(1, 0, 2).reshape(TOKENS, D_T)
    block = D_T // N_DP
    context_blocks = context.reshape(TOKENS, N_DP, block).transpose(1, 0, 2)
    out_blocks = teacher_out.reshape(N_DP, block, D_T)

    def add_block(total, pair):
        part = jnp.dot(pair[0], pair[1], preferred_element_type=jnp.float32).astype(jnp.bfloat16)
        part = lax.optimization_barrier(part)
        return (total + part.astype(jnp.float32), None)
    summed, _ = lax.scan(add_block, jnp.zeros((TOKENS, D_T), jnp.float32), (context_blocks, out_blocks))
    hidden = (teacher_resid.astype(jnp.float32) + summed).astype(jnp.bfloat16)
    target = jnp.dot(hidden, distill_proj, preferred_element_type=jnp.float32)
    state = student_resid.astype(jnp.float32) + jnp.dot(student_context, student_out, preferred_element_type=jnp.float32)
    inverse = lax.rsqrt(lax.optimization_barrier(jnp.mean(state * state, axis=1, keepdims=True)) + EPS)
    pred = state * inverse * student_gain
    error = (pred - target) * TOKENS ** (-0.5)
    upstream = error * student_gain
    inner = lax.optimization_barrier(jnp.mean(upstream * state, axis=1, keepdims=True))
    grad_state = inverse * upstream - state * inverse ** 3 * inner
    grad_wo = jnp.dot(student_context.T, grad_state.astype(jnp.bfloat16), preferred_element_type=jnp.float32).astype(jnp.bfloat16)
    grad_gain = lax.optimization_barrier(jnp.sum(error * state * inverse, axis=0))
    grad_proj = -jnp.dot(hidden.T, error.astype(jnp.bfloat16), preferred_element_type=jnp.float32)
    return (grad_wo, grad_gain, grad_proj)
```

```python
import jax
import jax.numpy as jnp
from jax import lax
from jax.sharding import PartitionSpec as P

HEADS = 64
KV_HEADS = 8
HEAD = 128


EPS = 1e-05


def on_device(
    teacher_query,
    teacher_keys,
    teacher_values,
    teacher_out,
    teacher_resid,
    distill_proj,
    student_context,
    student_resid,
    student_out,
    student_gain,
):
    groups = HEADS // KV_HEADS
    dp_index = lax.axis_index("dp")
    mp_index = lax.axis_index("mp")
    query_rows, query_width = teacher_query.shape
    local_heads = query_width // HEAD
    kv_local = max(local_heads // groups, 1)
    kv_start = dp_index * local_heads // groups
    key_mine = lax.dynamic_slice_in_dim(teacher_keys, kv_start * HEAD, kv_local * HEAD, 1)
    value_mine = lax.dynamic_slice_in_dim(teacher_values, kv_start * HEAD, kv_local * HEAD, 1)
    both = lax.all_gather(jnp.concatenate([key_mine, value_mine], 1), "mp", axis=0, tiled=True)
    keys_all, values_all = both[:, : kv_local * HEAD], both[:, kv_local * HEAD :]
    total = keys_all.shape[0]
    repeat = local_heads // kv_local
    queries = teacher_query.reshape(query_rows, kv_local, repeat, HEAD)
    keyed = keys_all.reshape(total, kv_local, HEAD)
    valued = values_all.reshape(total, kv_local, HEAD)
    scores = jnp.einsum(
        "qgrd,kgd->grqk", queries, keyed, preferred_element_type=jnp.float32
    ) * HEAD ** (-0.5)
    query_pos = mp_index * query_rows + lax.iota(jnp.int32, query_rows)
    key_pos = lax.iota(jnp.int32, total)
    allowed = query_pos[:, None] >= key_pos[None, :]
    scores = jnp.where(allowed, scores, -jnp.inf)
    top = jnp.max(scores, axis=-1, keepdims=True)
    weights = jnp.exp(scores - top)
    probs = (weights / jnp.sum(weights, axis=-1, keepdims=True)).astype(jnp.bfloat16)
    context = jnp.einsum("grqk,kgd->qgrd", probs, valued, preferred_element_type=jnp.float32)
    context = context.astype(jnp.bfloat16).reshape(query_rows, query_width)
    head_terms = jnp.dot(
        lax.all_gather(context, "mp", axis=0, tiled=True),
        teacher_out,
        preferred_element_type=jnp.float32,
    )
    summed = lax.psum_scatter(
        head_terms.astype(jnp.bfloat16), "dp", scatter_dimension=0, tiled=True
    ).astype(jnp.float32)
    hidden = (teacher_resid.astype(jnp.float32) + summed).astype(jnp.bfloat16)
    hidden_all = lax.all_gather(hidden, "dp", axis=0, tiled=True)
    student_all = lax.all_gather(student_context, "mp", axis=0, tiled=True)
    rows = hidden_all
    target = lax.psum_scatter(
        jnp.dot(rows, distill_proj, preferred_element_type=jnp.float32),
        "mp",
        scatter_dimension=0,
        tiled=True,
    )
    width = student_context.shape[1]
    columns = student_out.shape[1]
    state = student_resid.astype(jnp.float32) + jnp.dot(
        student_context, student_out, preferred_element_type=jnp.float32
    )
    grad_scale = total ** (-0.5)
    gain_mine = lax.dynamic_slice_in_dim(student_gain, dp_index * columns, columns, 0)
    squares = lax.psum(jnp.sum(state * state, axis=1), "dp")
    inverse = lax.rsqrt(squares / width + EPS)[:, None]
    pred = state * inverse * gain_mine
    error = (pred - target) * grad_scale
    upstream = error * gain_mine
    inner = lax.psum(jnp.sum(upstream * state, axis=1), "dp")
    grad_state = inverse * upstream - state * inverse**3 * (inner / width)[:, None]
    gain_term = error * state * inverse
    grad_bf = grad_state.astype(jnp.bfloat16)
    error_bf = error.astype(jnp.bfloat16)
    gain_sum = lax.psum(jnp.sum(gain_term, axis=0), "mp")
    contract_rows = (((0,), (0,)), ((), ()))
    grad_proj = -lax.dot_general(
        rows,
        lax.all_gather(error_bf, "mp", axis=0, tiled=True),
        contract_rows,
        preferred_element_type=jnp.float32,
    )
    grad_wo = lax.dot_general(
        student_all,
        lax.all_gather(grad_bf, "mp", axis=0, tiled=True),
        contract_rows,
        preferred_element_type=jnp.float32,
    ).astype(jnp.bfloat16)
    return (grad_wo, gain_sum, grad_proj)


def solution(mesh):
    in_specs = (
        P("mp", "dp"),
        P("mp", None),
        P("mp", None),
        P("dp", "mp"),
        P("dp", "mp"),
        P("mp", "dp"),
        P("mp", None),
        P("mp", "dp"),
        P(None, "dp"),
        P(),
    )
    out_specs = (P(None, "dp"), P("dp"), P("mp", "dp"))
    return jax.shard_map(
        on_device, mesh=mesh, in_specs=in_specs, out_specs=out_specs, check_vma=False
    )
```

```python
import functools

import jax
import jax.numpy as jnp
from jax import lax
from jax.experimental import pallas as pl
from jax.experimental.pallas import tpu as pltpu
from jax.sharding import PartitionSpec as P

HEADS = 64
KV_HEADS = 8
HEAD = 128
EPS = 1e-05
MESH = pl.DeviceIdType.MESH
F32 = jnp.float32
BF16 = jnp.bfloat16


def position_of(index, n):
    z, x = index // 2, index % 2
    return z + x * (n - 1 - 2 * z)


def index_at(position, n):
    side = position // (n // 2)
    return 2 * (position + side * (n - 1 - 2 * position)) + side


class Gather:
    def __init__(self, block, mine, mn, mp, sends, recvs, passes, own=None):
        self.block, self.mine, self.mn, self.mp, self.own = block, mine, mn, mp, own
        self.sends, self.recvs, self.passes = sends, recvs, passes
        self.core, self.group, self.groups = mp % 2, mp // 2, mn // 2
        self.sibling = self.group * 2 + (1 - self.core)

    def same(self, j):
        return ((self.group + j) % self.groups) * 2 + self.core

    def other(self, j):
        return ((self.group + j) % self.groups) * 2 + (1 - self.core)

    def copy(self, source, who, send_sem, target):
        return pltpu.make_async_remote_copy(
            src_ref=source,
            dst_ref=self.block(who),
            send_sem=send_sem,
            recv_sem=self.recvs.at[who],
            device_id={"mp": target},
            device_id_type=MESH,
        )

    def first(self, j):
        target = self.same(j) if j else self.sibling
        return self.copy(self.mine, self.mp, self.sends.at[j], target)

    def start(self):
        for j in range(self.groups):
            self.first(j).start()

    def passed(self, j):
        who = self.same(j)
        return self.copy(self.block(who), who, self.passes.at[j], self.sibling)

    def forward(self):
        for j in range(1, self.groups):
            self.passed(j).wait_recv()
            self.passed(j).start()

    def finish(self):
        for j in range(self.groups):
            who = self.other(j)
            self.copy(self.block(who), who, self.sends.at[j], self.sibling).wait_recv()
        for j in range(self.groups):
            self.first(j).wait_send()
        for j in range(1, self.groups):
            self.passed(j).wait_send()


def to_columns(row, rows, width):
    tile = jnp.transpose(jnp.broadcast_to(row, (128, rows)))
    return jnp.concatenate([tile] * (width // 128), axis=1) if width > 128 else tile


def sum_to_row(values):
    ones = jnp.ones((8, values.shape[1]), F32)
    return lax.dot_general(
        ones, values, (((1,), (1,)), ((), ())),
        precision=lax.Precision.HIGHEST, preferred_element_type=F32,
    )


def middle(
    n, mn, width, tokens,
    ctx, tout_hbm, resid, proj_hbm, sctx_hbm, sresid, sout_hbm, gain,
    hid_out, sall_out, err_out, st_out, coef_out,
    tout, proj, sctx, sout, head, hid, rs, tsend, trecv, err, st, state, sq, inn, coef,
    load, store, rs_send, rs_recv, ag_send, ag_recv, t_send, t_recv,
    sq_send, sq_recv, in_send, in_recv, co_send, co_recv,
    s_send, s_recv, s_pass, st_send, st_recv, st_pass, e_send, e_recv, e_pass,
):
    d, m = lax.axis_index("dp"), lax.axis_index("mp")
    rows = tokens // mn
    shard = tokens // n
    half = shard // 2
    per = n // mn
    features = proj.shape[0]
    columns = proj.shape[1]
    p = position_of(d, n)

    loads = [
        pltpu.make_async_copy(src, dst, load.at[i])
        for i, (src, dst) in enumerate(
            ((tout_hbm, tout), (sctx_hbm, sctx), (sout_hbm, sout), (proj_hbm, proj))
        )
    ]
    for one in loads:
        one.start()

    barrier = pltpu.get_barrier_semaphore()
    for j in range(1, n):
        pl.semaphore_signal(barrier, inc=1, device_id={"dp": (d + j) % n}, device_id_type=MESH)
    for j in range(1, mn):
        pl.semaphore_signal(barrier, inc=1, device_id={"mp": (m + j) % mn}, device_id_type=MESH)
    pl.semaphore_wait(barrier, n - 1 + mn - 1)

    def block_of(ref):
        return lambda who: ref.at[pl.ds(pl.multiple_of(who * rows, rows), rows), :]

    my_rows = pl.ds(pl.multiple_of(m * rows, rows), rows)
    student = Gather(block_of(sall_out), sctx_hbm, mn, m, s_send, s_recv, s_pass)
    student.start()
    keep = pltpu.make_async_copy(sctx_hbm, sall_out.at[my_rows, :], store.at[0])
    keep.start()

    loads[0].wait()
    tile = min(512, features)

    @pl.loop(0, features // tile)
    def _(i):
        cols = pl.ds(pl.multiple_of(i * tile, tile), tile)
        head[:, cols] = jnp.dot(ctx[...], tout[:, cols], preferred_element_type=F32).astype(BF16)

    def chunk(position, way):
        start = index_at(position, n) * shard + way * half
        return pl.ds(pl.multiple_of(start, half), half)

    def toward(way):
        return index_at((p + 1 - 2 * way + n) % n, n)

    def sign(way):
        return 1 - 2 * way

    def reduce_copy(s, way):
        c = (p - sign(way) * (s + 1) + 2 * n) % n
        return pltpu.make_async_remote_copy(
            src_ref=head.at[chunk(c, way), :],
            dst_ref=rs.at[way, s],
            send_sem=rs_send.at[way, s],
            recv_sem=rs_recv.at[way, s],
            device_id={"dp": toward(way)},
            device_id_type=MESH,
        )

    for way in (0, 1):
        reduce_copy(0, way).start()

    def exchange(buf, sends, recvs, j):
        return pltpu.make_async_remote_copy(
            src_ref=buf.at[d],
            dst_ref=buf.at[d],
            send_sem=sends.at[j],
            recv_sem=recvs.at[d],
            device_id={"dp": (d + j) % n},
            device_id_type=MESH,
        )

    def exchange_wait(buf, sends, recvs):
        for j in range(1, n):
            who = (d + j) % n
            pltpu.make_async_remote_copy(
                src_ref=buf.at[who], dst_ref=buf.at[who], send_sem=sends.at[j],
                recv_sem=recvs.at[who], device_id={"dp": who}, device_id_type=MESH,
            ).wait_recv()
        for j in range(1, n):
            exchange(buf, sends, recvs, j).wait_send()

    def total_of(buf):
        whole = buf[0]
        for j in range(1, n):
            whole = whole + buf[j]
        return whole

    def reduce_step(s):
        for way in (0, 1):
            reduce_copy(s - 1, way).wait_recv()
            c = (p - sign(way) * (s + 1) + 2 * n) % n
            where = chunk(c, way)
            head[where, :] = (head[where, :].astype(F32) + rs[way, s - 1].astype(F32)).astype(BF16)
            reduce_copy(s, way).start()

    reduce_step(1)

    loads[1].wait()
    loads[2].wait()
    state[...] = sresid[...].astype(F32) + jnp.dot(sctx[...], sout[...], preferred_element_type=F32)
    st[my_rows, :] = state[...].astype(BF16)
    sq[d] = sum_to_row(state[...] * state[...])
    for j in range(1, n):
        exchange(sq, sq_send, sq_recv, j).start()
    states = Gather(block_of(st), st.at[my_rows, :], mn, m, st_send, st_recv, st_pass)
    states.start()

    @pl.loop(2, n - 1)
    def _(s):
        reduce_step(s)

    for way in (0, 1):
        reduce_copy(n - 2, way).wait_recv()
        where = chunk(p, way)
        mine = pl.ds(way * half, half)
        summed = head[where, :].astype(F32) + rs[way, n - 2].astype(F32)
        hid[where, :] = (resid[mine, :].astype(F32) + summed).astype(BF16)

    def gather_copy(s, way):
        where = chunk((p - sign(way) * s + 2 * n) % n, way)
        return pltpu.make_async_remote_copy(
            src_ref=hid.at[where, :],
            dst_ref=hid.at[where, :],
            send_sem=ag_send.at[way, s],
            recv_sem=ag_recv.at[way, s],
            device_id={"dp": toward(way)},
            device_id_type=MESH,
        )

    def arrival(s, way):
        where = chunk((p - sign(way) * (s + 1) + 2 * n) % n, way)
        return pltpu.make_async_remote_copy(
            src_ref=hid.at[where, :],
            dst_ref=hid.at[where, :],
            send_sem=ag_send.at[way, s],
            recv_sem=ag_recv.at[way, s],
            device_id={"dp": toward(way)},
            device_id_type=MESH,
        )

    def target_copy(owner, way):
        to = owner // per
        piece = pl.ds(pl.multiple_of((owner % per) * shard + way * half, half), half)
        start = pl.ds(pl.multiple_of(owner * shard + way * half, half), half)
        return pltpu.make_async_remote_copy(
            src_ref=tsend.at[start, :],
            dst_ref=trecv.at[m, piece, :],
            send_sem=t_send.at[way, owner],
            recv_sem=t_recv.at[m, way, owner % per],
            device_id={"mp": to},
            device_id_type=MESH,
        )

    def project(s):
        where = [chunk((p - sign(way) * s + 2 * n) % n, way) for way in (0, 1)]
        both = jnp.concatenate([hid[w, :] for w in where], axis=0)
        out = jnp.dot(both, proj[...], preferred_element_type=F32).astype(BF16)
        for way in (0, 1):
            tsend[where[way], :] = out[way * half : (way + 1) * half]
            owner = index_at((p - sign(way) * s + 2 * n) % n, n)

            @pl.when(owner // per != m)
            def _():
                target_copy(owner, way).start()

    for way in (0, 1):
        gather_copy(0, way).start()
    loads[3].wait()
    student.forward()
    states.forward()
    project(0)

    @pl.loop(1, n - 1)
    def _(s):
        for way in (0, 1):
            arrival(s - 1, way).wait_recv()
            gather_copy(s, way).start()
        project(s)

    for way in (0, 1):
        arrival(n - 2, way).wait_recv()
    project(n - 1)
    hid_store = pltpu.make_async_copy(hid, hid_out, store.at[1])
    hid_store.start()

    exchange_wait(sq, sq_send, sq_recv)
    inverse_row = lax.rsqrt(total_of(sq) / width + EPS)
    inverse = to_columns(inverse_row[0:1], rows, columns)
    pred = state[...] * inverse * gain[...]

    target = tsend[my_rows, :].astype(F32)
    for j in range(1, mn):
        who = (m + j) % mn
        for way in (0, 1):
            for k in range(per):
                piece = pl.ds(k * shard + way * half, half)
                pltpu.make_async_remote_copy(
                    src_ref=trecv.at[who, piece, :],
                    dst_ref=trecv.at[who, piece, :],
                    send_sem=t_send.at[way, k],
                    recv_sem=t_recv.at[who, way, k],
                    device_id={"mp": who},
                    device_id_type=MESH,
                ).wait_recv()
        target = target + trecv[who].astype(F32)

    error = (pred - target) * (tokens ** -0.5)
    err[my_rows, :] = error.astype(BF16)
    errors = Gather(block_of(err), err.at[my_rows, :], mn, m, e_send, e_recv, e_pass)
    errors.start()
    inn[d] = sum_to_row(error * gain[...] * state[...])
    for j in range(1, n):
        exchange(inn, in_send, in_recv, j).start()

    states.finish()
    st_store = pltpu.make_async_copy(st, st_out, store.at[2])
    st_store.start()
    student.finish()

    exchange_wait(inn, in_send, in_recv)
    inner_row = total_of(inn)
    coef[m, 0:8, :] = inverse_row
    coef[m, 8:16, :] = inverse_row * inverse_row * inverse_row * (inner_row / width)

    def coef_copy(j):
        return pltpu.make_async_remote_copy(
            src_ref=coef.at[m], dst_ref=coef.at[m], send_sem=co_send.at[j],
            recv_sem=co_recv.at[m], device_id={"mp": (m + j) % mn}, device_id_type=MESH,
        )

    for j in range(1, mn):
        coef_copy(j).start()
    errors.forward()
    errors.finish()
    err_store = pltpu.make_async_copy(err, err_out, store.at[3])
    err_store.start()
    for j in range(1, mn):
        who = (m + j) % mn
        pltpu.make_async_remote_copy(
            src_ref=coef.at[who], dst_ref=coef.at[who], send_sem=co_send.at[j],
            recv_sem=co_recv.at[who], device_id={"mp": who}, device_id_type=MESH,
        ).wait_recv()
    for j in range(1, mn):
        coef_copy(j).wait_send()
    coef_out[...] = coef[...]

    @pl.loop(0, n - 1)
    def _(s):
        for way in (0, 1):
            reduce_copy(s, way).wait_send()
            gather_copy(s, way).wait_send()

    @pl.loop(0, n)
    def _(owner):
        @pl.when(owner // per != m)
        def _():
            for way in (0, 1):
                target_copy(owner, way).wait_send()

    keep.wait()
    hid_store.wait()
    st_store.wait()
    err_store.wait()


def on_device(
    n,
    mn,
    teacher_query,
    teacher_keys,
    teacher_values,
    teacher_out,
    teacher_resid,
    distill_proj,
    student_context,
    student_resid,
    student_out,
    student_gain,
):
    groups = HEADS // KV_HEADS
    dp_index = lax.axis_index("dp")
    mp_index = lax.axis_index("mp")
    query_rows, query_width = teacher_query.shape
    local_heads = query_width // HEAD
    kv_local = max(local_heads // groups, 1)
    kv_start = dp_index * local_heads // groups
    key_mine = lax.dynamic_slice_in_dim(teacher_keys, kv_start * HEAD, kv_local * HEAD, 1)
    value_mine = lax.dynamic_slice_in_dim(teacher_values, kv_start * HEAD, kv_local * HEAD, 1)
    both = lax.all_gather(jnp.concatenate([key_mine, value_mine], 1), "mp", axis=0, tiled=True)
    keys_all, values_all = both[:, : kv_local * HEAD], both[:, kv_local * HEAD :]
    total = keys_all.shape[0]
    repeat = local_heads // kv_local
    queries = teacher_query.reshape(query_rows, kv_local, repeat, HEAD)
    keyed = keys_all.reshape(total, kv_local, HEAD)
    valued = values_all.reshape(total, kv_local, HEAD)
    scores = jnp.einsum(
        "qgrd,kgd->grqk", queries, keyed, preferred_element_type=jnp.float32
    ) * HEAD ** (-0.5)
    query_pos = mp_index * query_rows + lax.iota(jnp.int32, query_rows)
    key_pos = lax.iota(jnp.int32, total)
    allowed = query_pos[:, None] >= key_pos[None, :]
    scores = jnp.where(allowed, scores, -jnp.inf)
    top = jnp.max(scores, axis=-1, keepdims=True)
    weights = jnp.exp(scores - top)
    probs = (weights / jnp.sum(weights, axis=-1, keepdims=True)).astype(jnp.bfloat16)
    context = jnp.einsum("grqk,kgd->qgrd", probs, valued, preferred_element_type=jnp.float32)
    context = context.astype(jnp.bfloat16).reshape(query_rows, query_width)
    context_all = lax.all_gather(context, "mp", axis=0, tiled=True)

    features, columns = distill_proj.shape
    width = student_context.shape[1]
    shard = total // n
    rows = total // mn
    gain = lax.dynamic_slice_in_dim(student_gain, dp_index * columns, columns, 0).reshape(1, columns)
    vmem = pl.BlockSpec(memory_space=pltpu.VMEM)
    anywhere = pl.BlockSpec(memory_space=pl.ANY)
    dma = pltpu.SemaphoreType.DMA
    pairs = mn // 2
    hidden, student_all, error, state, coef = pl.pallas_call(
        functools.partial(middle, n, mn, width, total),
        out_shape=(
            jax.ShapeDtypeStruct((total, features), BF16),
            jax.ShapeDtypeStruct((total, width), BF16),
            jax.ShapeDtypeStruct((total, columns), BF16),
            jax.ShapeDtypeStruct((total, columns), BF16),
            jax.ShapeDtypeStruct((mn, 16, rows), F32),
        ),
        in_specs=[vmem, anywhere, vmem, anywhere, anywhere, vmem, anywhere, vmem],
        out_specs=(anywhere, anywhere, anywhere, anywhere, vmem),
        scratch_shapes=[
            pltpu.VMEM(teacher_out.shape, BF16),
            pltpu.VMEM(distill_proj.shape, BF16),
            pltpu.VMEM(student_context.shape, BF16),
            pltpu.VMEM(student_out.shape, BF16),
            pltpu.VMEM((total, features), BF16),
            pltpu.VMEM((total, features), BF16),
            pltpu.VMEM((2, n - 1, shard // 2, features), BF16),
            pltpu.VMEM((total, columns), BF16),
            pltpu.VMEM((mn, rows, columns), BF16),
            pltpu.VMEM((total, columns), BF16),
            pltpu.VMEM((total, columns), BF16),
            pltpu.VMEM((rows, columns), F32),
            pltpu.VMEM((n, 8, rows), F32),
            pltpu.VMEM((n, 8, rows), F32),
            pltpu.VMEM((mn, 16, rows), F32),
            dma((4,)),
            dma((4,)),
            dma((2, n - 1)),
            dma((2, n - 1)),
            dma((2, n - 1)),
            dma((2, n - 1)),
            dma((2, n)),
            dma((mn, 2, n // mn)),
            dma((n,)), dma((n,)), dma((n,)), dma((n,)),
            dma((mn,)), dma((mn,)),
            dma((pairs,)), dma((mn,)), dma((pairs,)),
            dma((pairs,)), dma((mn,)), dma((pairs,)),
            dma((pairs,)), dma((mn,)), dma((pairs,)),
        ],
        compiler_params=pltpu.CompilerParams(
            collective_id=0, has_side_effects=True, vmem_limit_bytes=48 * 1024 * 1024
        ),
        name="middle",
    )(
        context_all, teacher_out, teacher_resid, distill_proj,
        student_context, student_resid, student_out, gain,
    )
    inverse = coef[:, 0, :].reshape(total, 1)
    pull = coef[:, 8, :].reshape(total, 1)
    wide = error.astype(F32) * inverse
    kept = state.astype(F32)
    grad_gain = jnp.sum(wide * kept, axis=0)
    grad_state = (wide * gain - kept * pull).astype(BF16)
    contract_rows = (((0,), (0,)), ((), ()))
    grad_proj = -lax.dot_general(hidden, error, contract_rows, preferred_element_type=F32)
    grad_wo = lax.dot_general(
        student_all, grad_state, contract_rows, preferred_element_type=F32
    ).astype(BF16)
    return (grad_wo, grad_gain, grad_proj)


def solution(mesh):
    in_specs = (
        P("mp", "dp"),
        P("mp", None),
        P("mp", None),
        P("dp", "mp"),
        P("dp", "mp"),
        P("mp", "dp"),
        P("mp", None),
        P("mp", "dp"),
        P(None, "dp"),
        P(),
    )
    out_specs = (P(None, "dp"), P("dp"), P("mp", "dp"))
    return jax.shard_map(
        functools.partial(on_device, mesh.shape["dp"], mesh.shape["mp"]),
        mesh=mesh, in_specs=in_specs, out_specs=out_specs, check_vma=False,
    )
```

```python
import functools

import jax
import jax.numpy as jnp
from jax import lax
from jax.experimental import pallas as pl
from jax.experimental.pallas import tpu as pltpu
from jax.sharding import PartitionSpec as P

HEADS = 64
KV_HEADS = 8
HEAD = 128
PIECES = 4
EPS = 1e-05
MESH = pl.DeviceIdType.MESH
F32 = jnp.float32
BF16 = jnp.bfloat16


def position_of(index, n):
    z, x = index // 2, index % 2
    return z + x * (n - 1 - 2 * z)


def index_at(position, n):
    side = position // (n // 2)
    return 2 * (position + side * (n - 1 - 2 * position)) + side


class Gather:
    def __init__(self, block, mine, mn, mp, sends, recvs, passes, own=None):
        self.block, self.mine, self.mn, self.mp, self.own = block, mine, mn, mp, own
        self.sends, self.recvs, self.passes = sends, recvs, passes
        self.core, self.group, self.groups = mp % 2, mp // 2, mn // 2
        self.sibling = self.group * 2 + (1 - self.core)

    def same(self, j):
        return ((self.group + j) % self.groups) * 2 + self.core

    def other(self, j):
        return ((self.group + j) % self.groups) * 2 + (1 - self.core)

    def copy(self, source, who, send_sem, target):
        return pltpu.make_async_remote_copy(
            src_ref=source,
            dst_ref=self.block(who),
            send_sem=send_sem,
            recv_sem=self.recvs.at[who],
            device_id={"mp": target},
            device_id_type=MESH,
        )

    def first(self, j):
        target = self.same(j) if j else self.sibling
        return self.copy(self.mine, self.mp, self.sends.at[j], target)

    def start(self):
        for j in range(self.groups):
            self.first(j).start()

    def passed(self, j):
        who = self.same(j)
        return self.copy(self.block(who), who, self.passes.at[j], self.sibling)

    def forward(self):
        for j in range(1, self.groups):
            self.passed(j).wait_recv()
            self.passed(j).start()

    def finish(self):
        for j in range(self.groups):
            who = self.other(j)
            self.copy(self.block(who), who, self.sends.at[j], self.sibling).wait_recv()
        for j in range(self.groups):
            self.first(j).wait_send()
        for j in range(1, self.groups):
            self.passed(j).wait_send()


def to_columns(row, rows, width):
    tile = jnp.transpose(jnp.broadcast_to(row, (128, rows)))
    return jnp.concatenate([tile] * (width // 128), axis=1) if width > 128 else tile


def sum_to_row(values):
    ones = jnp.ones((8, values.shape[1]), F32)
    return lax.dot_general(
        ones, values, (((1,), (1,)), ((), ())),
        precision=lax.Precision.HIGHEST, preferred_element_type=F32,
    )


def middle(
    n, mn, width, tokens,
    query, keys_hbm, values_hbm, tout_hbm, resid, proj_hbm, sctx_hbm, sresid, sout_hbm, gains,
    hid_out, sall_out, err_out, st_out, coef_out, gain_out,
    kv, ctx, tout, proj, sctx, sout, head, hid, rs, tsend, trecv, err, st, state, sq, inn, coef,
    load, store, rs_send, rs_recv, ag_send, ag_recv, t_send, t_recv,
    sq_send, sq_recv, in_send, in_recv, co_send, co_recv,
    k_send, k_recv, k_pass, c_send, c_recv, c_pass,
    s_send, s_recv, s_pass, st_send, st_recv, st_pass, e_send, e_recv, e_pass,
):
    d, m = lax.axis_index("dp"), lax.axis_index("mp")
    rows = tokens // mn
    shard = tokens // n
    half = shard // 2
    per = n // mn
    features, columns = proj.shape
    piece = features // PIECES
    heads = query.shape[1] // HEAD
    p = position_of(d, n)
    my_rows = pl.ds(pl.multiple_of(m * rows, rows), rows)

    kv_cols = pl.ds(pl.multiple_of((d * heads // (HEADS // KV_HEADS)) * HEAD, HEAD), HEAD)
    loads = [
        pltpu.make_async_copy(src, dst, load.at[i])
        for i, (src, dst) in enumerate(
            (
                (keys_hbm.at[:, kv_cols], kv.at[my_rows, 0:HEAD]),
                (values_hbm.at[:, kv_cols], kv.at[my_rows, HEAD : 2 * HEAD]),
                (sctx_hbm, sctx),
                (sout_hbm, sout),
                (tout_hbm, tout),
                (proj_hbm, proj),
            )
        )
    ]
    for one in loads:
        one.start()

    barrier = pltpu.get_barrier_semaphore()
    for j in range(1, n):
        pl.semaphore_signal(barrier, inc=1, device_id={"dp": (d + j) % n}, device_id_type=MESH)
    for j in range(1, mn):
        pl.semaphore_signal(barrier, inc=1, device_id={"mp": (m + j) % mn}, device_id_type=MESH)
    pl.semaphore_wait(barrier, n - 1 + mn - 1)

    def block_of(ref, cols=slice(None)):
        return lambda who: ref.at[pl.ds(pl.multiple_of(who * rows, rows), rows), cols]

    loads[0].wait()
    loads[1].wait()
    pair = Gather(block_of(kv), kv.at[my_rows, :], mn, m, k_send, k_recv, k_pass)
    pair.start()

    def exchange(buf, sends, recvs, j):
        return pltpu.make_async_remote_copy(
            src_ref=buf.at[d],
            dst_ref=buf.at[d],
            send_sem=sends.at[j],
            recv_sem=recvs.at[d],
            device_id={"dp": (d + j) % n},
            device_id_type=MESH,
        )

    def exchange_wait(buf, sends, recvs):
        for j in range(1, n):
            who = (d + j) % n
            pltpu.make_async_remote_copy(
                src_ref=buf.at[who], dst_ref=buf.at[who], send_sem=sends.at[j],
                recv_sem=recvs.at[who], device_id={"dp": who}, device_id_type=MESH,
            ).wait_recv()
        for j in range(1, n):
            exchange(buf, sends, recvs, j).wait_send()

    def total_of(buf):
        whole = buf[0]
        for j in range(1, n):
            whole = whole + buf[j]
        return whole

    loads[2].wait()
    loads[3].wait()
    state[...] = sresid[...].astype(F32) + jnp.dot(sctx[...], sout[...], preferred_element_type=F32)
    pair.forward()
    st[my_rows, :] = state[...].astype(BF16)
    sq[d] = sum_to_row(state[...] * state[...])
    gain = gains[:, pl.ds(pl.multiple_of(d * columns, columns), columns)]
    gain_out[...] = gain
    pair.finish()

    query_pos = m * rows + lax.broadcasted_iota(jnp.int32, (rows, tokens), 0)
    allowed = query_pos >= lax.broadcasted_iota(jnp.int32, (rows, tokens), 1)
    keys, values = kv[:, 0:HEAD], kv[:, HEAD : 2 * HEAD]
    contexts = []
    for part in range(2):
        for h in range(part * heads // 2, (part + 1) * heads // 2):
            cols = slice(h * HEAD, (h + 1) * HEAD)
            scores = lax.dot_general(
                query[:, cols], keys, (((1,), (1,)), ((), ())), preferred_element_type=F32
            ) * HEAD ** (-0.5)
            scores = jnp.where(allowed, scores, -jnp.inf)
            weights = jnp.exp(scores - jnp.max(scores, axis=1, keepdims=True))
            whole = jnp.sum(weights, axis=1, keepdims=True)
            mixed = jnp.dot(weights.astype(BF16), values, preferred_element_type=F32)
            ctx[my_rows, cols] = (mixed / whole).astype(BF16)
        cols = slice(part * heads // 2 * HEAD, (part + 1) * heads // 2 * HEAD)
        contexts.append(
            Gather(
                block_of(ctx, cols), ctx.at[my_rows, cols], mn, m,
                c_send.at[part], c_recv.at[part], c_pass.at[part],
            )
        )
        contexts[part].start()
    for part in range(2):
        contexts[part].forward()
    for j in range(1, n):
        exchange(sq, sq_send, sq_recv, j).start()
    student = Gather(block_of(sall_out), sctx_hbm, mn, m, s_send, s_recv, s_pass)
    student.start()
    keep = pltpu.make_async_copy(sctx_hbm, sall_out.at[my_rows, :], store.at[0])
    keep.start()
    states = Gather(block_of(st), st.at[my_rows, :], mn, m, st_send, st_recv, st_pass)
    states.start()
    loads[4].wait()
    for part in range(2):
        contexts[part].finish()

    def chunk(position, way):
        start = index_at(position, n) * shard + way * half
        return pl.ds(pl.multiple_of(start, half), half)

    def toward(way):
        return index_at((p + 1 - 2 * way + n) % n, n)

    def at(way, s):
        return (p - (1 - 2 * way) * s + 2 * n) % n

    def cut(k):
        return slice(k * piece, (k + 1) * piece)

    def reduce_copy(s, way, k):
        return pltpu.make_async_remote_copy(
            src_ref=head.at[chunk(at(way, s + 1), way), cut(k)],
            dst_ref=rs.at[way, s, k],
            send_sem=rs_send.at[way, s, k],
            recv_sem=rs_recv.at[way, s, k],
            device_id={"dp": toward(way)},
            device_id_type=MESH,
        )

    for k in range(PIECES):
        head[:, cut(k)] = jnp.dot(
            ctx[...], tout[:, cut(k)], preferred_element_type=F32
        ).astype(BF16)
        for way in (0, 1):
            reduce_copy(0, way, k).start()

    @pl.loop(1, n - 1)
    def _(s):
        for k in range(PIECES):
            for way in (0, 1):
                where = chunk(at(way, s + 1), way)
                reduce_copy(s - 1, way, k).wait_recv()
                summed = head[where, cut(k)].astype(F32) + rs[way, s - 1, k].astype(F32)
                head[where, cut(k)] = summed.astype(BF16)
                reduce_copy(s, way, k).start()

    def moving(s, way, k, where):
        return pltpu.make_async_remote_copy(
            src_ref=hid.at[where, cut(k)],
            dst_ref=hid.at[where, cut(k)],
            send_sem=ag_send.at[way, s, k],
            recv_sem=ag_recv.at[way, s, k],
            device_id={"dp": toward(way)},
            device_id_type=MESH,
        )

    def gather_copy(s, way, k):
        return moving(s, way, k, chunk(at(way, s), way))

    def arrival(s, way, k):
        return moving(s, way, k, chunk(at(way, s + 1), way))

    for k in range(PIECES):
        for way in (0, 1):
            reduce_copy(n - 2, way, k).wait_recv()
            where = chunk(p, way)
            mine = pl.ds(way * half, half)
            summed = head[where, cut(k)].astype(F32) + rs[way, n - 2, k].astype(F32)
            hid[where, cut(k)] = (resid[mine, cut(k)].astype(F32) + summed).astype(BF16)
            gather_copy(0, way, k).start()

    def target_copy(owner, way):
        to = owner // per
        place = pl.ds(pl.multiple_of((owner % per) * shard + way * half, half), half)
        start = pl.ds(pl.multiple_of(owner * shard + way * half, half), half)
        return pltpu.make_async_remote_copy(
            src_ref=tsend.at[start, :],
            dst_ref=trecv.at[m, place, :],
            send_sem=t_send.at[way, owner],
            recv_sem=t_recv.at[m, way, owner % per],
            device_id={"mp": to},
            device_id_type=MESH,
        )

    def project(s, arrive, forward):
        where = [chunk(at(way, s), way) for way in (0, 1)]
        out = None
        for k in range(PIECES):
            for way in (0, 1):
                if arrive:
                    arrival(s - 1, way, k).wait_recv()
                if forward:
                    gather_copy(s, way, k).start()
            both = jnp.concatenate([hid[w, cut(k)] for w in where], axis=0)
            term = jnp.dot(both, proj[cut(k), :], preferred_element_type=F32)
            out = term if out is None else out + term
        out = out.astype(BF16)
        for way in (0, 1):
            tsend[where[way], :] = out[way * half : (way + 1) * half]
            owner = index_at(at(way, s), n)

            @pl.when(owner // per != m)
            def _():
                target_copy(owner, way).start()

    loads[5].wait()
    project(0, False, False)

    @pl.loop(1, n - 1)
    def _(s):
        project(s, True, True)

    project(n - 1, True, False)
    hid_store = pltpu.make_async_copy(hid, hid_out, store.at[1])
    hid_store.start()
    states.forward()
    student.forward()

    exchange_wait(sq, sq_send, sq_recv)
    inverse_row = lax.rsqrt(total_of(sq) / width + EPS)
    inverse = to_columns(inverse_row[0:1], rows, columns)
    pred = state[...] * inverse * gain

    target = tsend[my_rows, :].astype(F32)
    for j in range(1, mn):
        who = (m + j) % mn
        for way in (0, 1):
            for k in range(per):
                place = pl.ds(k * shard + way * half, half)
                pltpu.make_async_remote_copy(
                    src_ref=trecv.at[who, place, :],
                    dst_ref=trecv.at[who, place, :],
                    send_sem=t_send.at[way, k],
                    recv_sem=t_recv.at[who, way, k],
                    device_id={"mp": who},
                    device_id_type=MESH,
                ).wait_recv()
        target = target + trecv[who].astype(F32)

    error = (pred - target) * (tokens ** -0.5)
    err[my_rows, :] = error.astype(BF16)
    errors = Gather(block_of(err), err.at[my_rows, :], mn, m, e_send, e_recv, e_pass)
    errors.start()
    inn[d] = sum_to_row(error * gain * state[...])
    for j in range(1, n):
        exchange(inn, in_send, in_recv, j).start()

    states.finish()
    st_store = pltpu.make_async_copy(st, st_out, store.at[2])
    st_store.start()

    exchange_wait(inn, in_send, in_recv)
    inner_row = total_of(inn)
    coef[m, 0:8, :] = inverse_row
    coef[m, 8:16, :] = inverse_row * inverse_row * inverse_row * (inner_row / width)

    def coef_copy(j):
        return pltpu.make_async_remote_copy(
            src_ref=coef.at[m], dst_ref=coef.at[m], send_sem=co_send.at[j],
            recv_sem=co_recv.at[m], device_id={"mp": (m + j) % mn}, device_id_type=MESH,
        )

    for j in range(1, mn):
        coef_copy(j).start()
    errors.forward()
    student.finish()
    errors.finish()
    err_store = pltpu.make_async_copy(err, err_out, store.at[3])
    err_store.start()
    for j in range(1, mn):
        who = (m + j) % mn
        pltpu.make_async_remote_copy(
            src_ref=coef.at[who], dst_ref=coef.at[who], send_sem=co_send.at[j],
            recv_sem=co_recv.at[who], device_id={"mp": who}, device_id_type=MESH,
        ).wait_recv()
    for j in range(1, mn):
        coef_copy(j).wait_send()
    coef_out[...] = coef[...]

    @pl.loop(0, n - 1)
    def _(s):
        for way in (0, 1):
            for k in range(PIECES):
                reduce_copy(s, way, k).wait_send()
                gather_copy(s, way, k).wait_send()

    @pl.loop(0, n)
    def _(owner):
        @pl.when(owner // per != m)
        def _():
            for way in (0, 1):
                target_copy(owner, way).wait_send()

    keep.wait()
    hid_store.wait()
    st_store.wait()
    err_store.wait()


def on_device(
    n,
    mn,
    teacher_query,
    teacher_keys,
    teacher_values,
    teacher_out,
    teacher_resid,
    distill_proj,
    student_context,
    student_resid,
    student_out,
    student_gain,
):
    features, columns = distill_proj.shape
    width = student_context.shape[1]
    rows = teacher_query.shape[0]
    total = rows * mn
    shard = total // n
    vmem = pl.BlockSpec(memory_space=pltpu.VMEM)
    anywhere = pl.BlockSpec(memory_space=pl.ANY)
    dma = pltpu.SemaphoreType.DMA
    pairs = mn // 2
    hidden, student_all, error, state, coef, gain = pl.pallas_call(
        functools.partial(middle, n, mn, width, total),
        out_shape=(
            jax.ShapeDtypeStruct((total, features), BF16),
            jax.ShapeDtypeStruct((total, width), BF16),
            jax.ShapeDtypeStruct((total, columns), BF16),
            jax.ShapeDtypeStruct((total, columns), BF16),
            jax.ShapeDtypeStruct((mn, 16, rows), F32),
            jax.ShapeDtypeStruct((1, columns), F32),
        ),
        in_specs=[
            vmem, anywhere, anywhere, anywhere, vmem, anywhere, anywhere, vmem, anywhere, vmem,
        ],
        out_specs=(anywhere, anywhere, anywhere, anywhere, vmem, vmem),
        scratch_shapes=[
            pltpu.VMEM((total, 2 * HEAD), BF16),
            pltpu.VMEM((total, teacher_query.shape[1]), BF16),
            pltpu.VMEM(teacher_out.shape, BF16),
            pltpu.VMEM(distill_proj.shape, BF16),
            pltpu.VMEM(student_context.shape, BF16),
            pltpu.VMEM(student_out.shape, BF16),
            pltpu.VMEM((total, features), BF16),
            pltpu.VMEM((total, features), BF16),
            pltpu.VMEM((2, n - 1, PIECES, shard // 2, features // PIECES), BF16),
            pltpu.VMEM((total, columns), BF16),
            pltpu.VMEM((mn, rows, columns), BF16),
            pltpu.VMEM((total, columns), BF16),
            pltpu.VMEM((total, columns), BF16),
            pltpu.VMEM((rows, columns), F32),
            pltpu.VMEM((n, 8, rows), F32),
            pltpu.VMEM((n, 8, rows), F32),
            pltpu.VMEM((mn, 16, rows), F32),
            dma((6,)),
            dma((4,)),
            dma((2, n - 1, PIECES)),
            dma((2, n - 1, PIECES)),
            dma((2, n - 1, PIECES)),
            dma((2, n - 1, PIECES)),
            dma((2, n)),
            dma((mn, 2, n // mn)),
            dma((n,)), dma((n,)), dma((n,)), dma((n,)),
            dma((mn,)), dma((mn,)),
            dma((pairs,)), dma((mn,)), dma((pairs,)),
            dma((2, pairs)), dma((2, mn)), dma((2, pairs)),
            dma((pairs,)), dma((mn,)), dma((pairs,)),
            dma((pairs,)), dma((mn,)), dma((pairs,)),
            dma((pairs,)), dma((mn,)), dma((pairs,)),
        ],
        compiler_params=pltpu.CompilerParams(
            collective_id=0, has_side_effects=True, vmem_limit_bytes=48 * 1024 * 1024
        ),
        name="middle",
    )(
        teacher_query, teacher_keys, teacher_values, teacher_out, teacher_resid, distill_proj,
        student_context, student_resid, student_out, student_gain.reshape(1, width),
    )
    inverse = coef[:, 0, :].reshape(total, 1)
    pull = coef[:, 8, :].reshape(total, 1)
    wide = error.astype(F32) * inverse
    kept = state.astype(F32)
    grad_gain = jnp.sum(wide * kept, axis=0)
    grad_state = (wide * gain - kept * pull).astype(BF16)
    contract_rows = (((0,), (0,)), ((), ()))
    grad_proj = -lax.dot_general(hidden, error, contract_rows, preferred_element_type=F32)
    grad_wo = lax.dot_general(
        student_all, grad_state, contract_rows, preferred_element_type=F32
    ).astype(BF16)
    return (grad_wo, grad_gain, grad_proj)


def solution(mesh):
    in_specs = (
        P("mp", "dp"),
        P("mp", None),
        P("mp", None),
        P("dp", "mp"),
        P("dp", "mp"),
        P("mp", "dp"),
        P("mp", None),
        P("mp", "dp"),
        P(None, "dp"),
        P(),
    )
    out_specs = (P(None, "dp"), P("dp"), P("mp", "dp"))
    return jax.shard_map(
        functools.partial(on_device, mesh.shape["dp"], mesh.shape["mp"]),
        mesh=mesh, in_specs=in_specs, out_specs=out_specs, check_vma=False,
    )
```

```python
import functools

import jax
import jax.numpy as jnp
from jax import lax
from jax.experimental import pallas as pl
from jax.experimental.pallas import tpu as pltpu
from jax.sharding import PartitionSpec as P

HEADS = 64
KV_HEADS = 8
HEAD = 128
PIECES = 4
STEPS = 4
VMEM_BYTES = 56 * 1024 * 1024
EPS = 1e-05
MESH = pl.DeviceIdType.MESH
F32 = jnp.float32
BF16 = jnp.bfloat16


def position_of(index, n):
    z, x = index // 2, index % 2
    return z + x * (n - 1 - 2 * z)


def index_at(position, n):
    side = position // (n // 2)
    return 2 * (position + side * (n - 1 - 2 * position)) + side


class Gather:
    def __init__(self, block, mine, mn, mp, sends, recvs, passes, own=None):
        self.block, self.mine, self.mn, self.mp, self.own = block, mine, mn, mp, own
        self.sends, self.recvs, self.passes = sends, recvs, passes
        self.core, self.group, self.groups = mp % 2, mp // 2, mn // 2
        self.sibling = self.group * 2 + (1 - self.core)

    def same(self, j):
        return ((self.group + j) % self.groups) * 2 + self.core

    def other(self, j):
        return ((self.group + j) % self.groups) * 2 + (1 - self.core)

    def copy(self, source, who, send_sem, target):
        return pltpu.make_async_remote_copy(
            src_ref=source,
            dst_ref=self.block(who),
            send_sem=send_sem,
            recv_sem=self.recvs.at[who],
            device_id={"mp": target},
            device_id_type=MESH,
        )

    def first(self, j):
        target = self.same(j) if j else self.sibling
        return self.copy(self.mine, self.mp, self.sends.at[j], target)

    def start(self):
        for j in range(self.groups):
            self.first(j).start()

    def passed(self, j):
        who = self.same(j)
        return self.copy(self.block(who), who, self.passes.at[j], self.sibling)

    def forward(self):
        for j in range(1, self.groups):
            self.passed(j).wait_recv()
            self.passed(j).start()

    def finish(self):
        for j in range(self.groups):
            who = self.other(j)
            self.copy(self.block(who), who, self.sends.at[j], self.sibling).wait_recv()
        for j in range(self.groups):
            self.first(j).wait_send()
        for j in range(1, self.groups):
            self.passed(j).wait_send()


def to_columns(row, rows, width):
    tile = jnp.transpose(jnp.broadcast_to(row, (128, rows)))
    return jnp.concatenate([tile] * (width // 128), axis=1) if width > 128 else tile


def sum_to_row(values):
    ones = jnp.ones((8, values.shape[1]), F32)
    return lax.dot_general(
        ones, values, (((1,), (1,)), ((), ())),
        precision=lax.Precision.HIGHEST, preferred_element_type=F32,
    )


def middle(
    n, mn, width, tokens,
    query_hbm, keys_hbm, values_hbm, tout_hbm, resid_hbm, proj_hbm, sctx_hbm, sresid_hbm, sout_hbm,
    gain_hbm,
    hid_out, sall, err_out, st_out, coef_out, gain_out,
    hid, err, st, coef, gain_ref, sctx, query, resid, sresid,
    kv, ctx, tout, proj, sout, head, rs, tsend, trecv, state, sq, inn,
    load, store, rs_send, rs_recv, ag_send, ag_recv, t_send, t_recv,
    sq_send, sq_recv, in_send, in_recv, co_send, co_recv,
    k_send, k_recv, k_pass, c_send, c_recv, c_pass,
    s_send, s_recv, s_pass, st_send, st_recv, st_pass, e_send, e_recv, e_pass,
):
    d, m = lax.axis_index("dp"), lax.axis_index("mp")
    rows = tokens // mn
    shard = tokens // n
    half = shard // 2
    per = n // mn
    features, columns = proj.shape
    piece = features // PIECES
    heads = query.shape[1] // HEAD
    p = position_of(d, n)
    my_rows = pl.ds(pl.multiple_of(m * rows, rows), rows)

    kv_cols = pl.ds(pl.multiple_of((d * heads // (HEADS // KV_HEADS)) * HEAD, HEAD), HEAD)
    gain_cols = pl.ds(pl.multiple_of(d * columns, columns), columns)
    loads = [
        pltpu.make_async_copy(src, dst, load.at[i])
        for i, (src, dst) in enumerate(
            (
                (keys_hbm.at[:, kv_cols], kv.at[my_rows, 0:HEAD]),
                (values_hbm.at[:, kv_cols], kv.at[my_rows, HEAD : 2 * HEAD]),
                (sctx_hbm, sctx),
                (sout_hbm, sout),
                (tout_hbm, tout),
                (proj_hbm, proj),
                (query_hbm, query),
                (resid_hbm, resid),
                (sresid_hbm, sresid),
                (gain_hbm.at[:, gain_cols], gain_ref),
            )
        )
    ]
    for one in loads:
        one.start()

    barrier = pltpu.get_barrier_semaphore()
    for j in range(1, n):
        pl.semaphore_signal(barrier, inc=1, device_id={"dp": (d + j) % n}, device_id_type=MESH)
    for j in range(1, mn):
        pl.semaphore_signal(barrier, inc=1, device_id={"mp": (m + j) % mn}, device_id_type=MESH)
    pl.semaphore_wait(barrier, n - 1 + mn - 1)

    def block_of(ref, cols=slice(None)):
        return lambda who: ref.at[pl.ds(pl.multiple_of(who * rows, rows), rows), cols]

    loads[0].wait()
    loads[1].wait()
    pair = Gather(block_of(kv), kv.at[my_rows, :], mn, m, k_send, k_recv, k_pass)
    pair.start()

    def exchange(buf, sends, recvs, j):
        return pltpu.make_async_remote_copy(
            src_ref=buf.at[d],
            dst_ref=buf.at[d],
            send_sem=sends.at[j],
            recv_sem=recvs.at[d],
            device_id={"dp": (d + j) % n},
            device_id_type=MESH,
        )

    def exchange_wait(buf, sends, recvs):
        for j in range(1, n):
            who = (d + j) % n
            pltpu.make_async_remote_copy(
                src_ref=buf.at[who], dst_ref=buf.at[who], send_sem=sends.at[j],
                recv_sem=recvs.at[who], device_id={"dp": who}, device_id_type=MESH,
            ).wait_recv()
        for j in range(1, n):
            exchange(buf, sends, recvs, j).wait_send()

    def total_of(buf):
        whole = buf[0]
        for j in range(1, n):
            whole = whole + buf[j]
        return whole

    loads[2].wait()
    loads[3].wait()
    loads[8].wait()
    loads[9].wait()
    state[...] = sresid[...].astype(F32) + jnp.dot(sctx[...], sout[...], preferred_element_type=F32)
    pair.forward()
    st[my_rows, :] = state[...].astype(BF16)
    sq[d] = sum_to_row(state[...] * state[...])
    gain = gain_ref[...]
    pair.finish()
    loads[6].wait()

    query_pos = m * rows + lax.broadcasted_iota(jnp.int32, (rows, tokens), 0)
    allowed = query_pos >= lax.broadcasted_iota(jnp.int32, (rows, tokens), 1)
    keys, values = kv[:, 0:HEAD], kv[:, HEAD : 2 * HEAD]
    contexts = []
    for part in range(2):
        for h in range(part * heads // 2, (part + 1) * heads // 2):
            cols = slice(h * HEAD, (h + 1) * HEAD)
            scores = lax.dot_general(
                query[:, cols], keys, (((1,), (1,)), ((), ())), preferred_element_type=F32
            ) * HEAD ** (-0.5)
            scores = jnp.where(allowed, scores, -jnp.inf)
            weights = jnp.exp(scores - jnp.max(scores, axis=1, keepdims=True))
            whole = jnp.sum(weights, axis=1, keepdims=True)
            mixed = jnp.dot(weights.astype(BF16), values, preferred_element_type=F32)
            ctx[my_rows, cols] = (mixed / whole).astype(BF16)
        cols = slice(part * heads // 2 * HEAD, (part + 1) * heads // 2 * HEAD)
        contexts.append(
            Gather(
                block_of(ctx, cols), ctx.at[my_rows, cols], mn, m,
                c_send.at[part], c_recv.at[part], c_pass.at[part],
            )
        )
        contexts[part].start()
    for part in range(2):
        contexts[part].forward()
    for j in range(1, n):
        exchange(sq, sq_send, sq_recv, j).start()
    student = Gather(block_of(sall), sctx, mn, m, s_send, s_recv, s_pass)
    student.start()
    stores = [
        pltpu.make_async_copy(src, dst, store.at[i])
        for i, (src, dst) in enumerate(
            (
                (sctx, sall.at[my_rows, :]),
                (gain_ref, gain_out),
                (hid, hid_out),
                (st, st_out),
                (err, err_out),
                (coef, coef_out),
            )
        )
    ]
    stores[0].start()
    stores[1].start()
    states = Gather(block_of(st), st.at[my_rows, :], mn, m, st_send, st_recv, st_pass)
    states.start()
    loads[4].wait()
    for part in range(2):
        contexts[part].finish()

    def chunk(position, way):
        start = index_at(position, n) * shard + way * half
        return pl.ds(pl.multiple_of(start, half), half)

    def toward(way):
        return index_at((p + 1 - 2 * way + n) % n, n)

    def at(way, s):
        return (p - (1 - 2 * way) * s + 2 * n) % n

    def cut(k):
        return slice(k * piece, (k + 1) * piece)

    def reduce_copy(s, way, k):
        return pltpu.make_async_remote_copy(
            src_ref=head.at[chunk(at(way, s + 1), way), cut(k)],
            dst_ref=rs.at[way, s, k],
            send_sem=rs_send.at[way, s, k],
            recv_sem=rs_recv.at[way, s, k],
            device_id={"dp": toward(way)},
            device_id_type=MESH,
        )

    for k in range(PIECES):
        head[:, cut(k)] = jnp.dot(
            ctx[...], tout[:, cut(k)], preferred_element_type=F32
        ).astype(BF16)
        for way in (0, 1):
            reduce_copy(0, way, k).start()

    @pl.loop(1, n - 1)
    def _(s):
        for k in range(PIECES):
            for way in (0, 1):
                where = chunk(at(way, s + 1), way)
                reduce_copy(s - 1, way, k).wait_recv()
                summed = head[where, cut(k)].astype(F32) + rs[way, s - 1, k].astype(F32)
                head[where, cut(k)] = summed.astype(BF16)
                reduce_copy(s, way, k).start()

    def moving(s, way, k, where):
        return pltpu.make_async_remote_copy(
            src_ref=hid.at[where, cut(k)],
            dst_ref=hid.at[where, cut(k)],
            send_sem=ag_send.at[way, s, k],
            recv_sem=ag_recv.at[way, s, k],
            device_id={"dp": toward(way)},
            device_id_type=MESH,
        )

    def gather_copy(s, way, k):
        return moving(s, way, k, chunk(at(way, s), way))

    def arrival(s, way, k):
        return moving(s, way, k, chunk(at(way, s + 1), way))

    loads[7].wait()
    for k in range(PIECES):
        for way in (0, 1):
            reduce_copy(n - 2, way, k).wait_recv()
            where = chunk(p, way)
            mine = pl.ds(way * half, half)
            summed = head[where, cut(k)].astype(F32) + rs[way, n - 2, k].astype(F32)
            hid[where, cut(k)] = (resid[mine, cut(k)].astype(F32) + summed).astype(BF16)
            gather_copy(0, way, k).start()

    def target_copy(owner, way):
        to = owner // per
        place = pl.ds(pl.multiple_of((owner % per) * shard + way * half, half), half)
        start = pl.ds(pl.multiple_of(owner * shard + way * half, half), half)
        return pltpu.make_async_remote_copy(
            src_ref=tsend.at[start, :],
            dst_ref=trecv.at[m, place, :],
            send_sem=t_send.at[way, owner],
            recv_sem=t_recv.at[m, way, owner % per],
            device_id={"mp": to},
            device_id_type=MESH,
        )

    def project(s, arrive, forward):
        where = [chunk(at(way, s), way) for way in (0, 1)]
        out = None
        for k in range(PIECES):
            for way in (0, 1):
                if arrive:
                    arrival(s - 1, way, k).wait_recv()
                if forward:
                    gather_copy(s, way, k).start()
            both = jnp.concatenate([hid[w, cut(k)] for w in where], axis=0)
            term = jnp.dot(both, proj[cut(k), :], preferred_element_type=F32)
            out = term if out is None else out + term
        out = out.astype(BF16)
        for way in (0, 1):
            tsend[where[way], :] = out[way * half : (way + 1) * half]
            owner = index_at(at(way, s), n)

            @pl.when(owner // per != m)
            def _():
                target_copy(owner, way).start()

    loads[5].wait()
    project(0, False, False)

    @pl.loop(1, n - 1)
    def _(s):
        project(s, True, True)

    project(n - 1, True, False)
    stores[2].start()
    states.forward()
    student.forward()

    exchange_wait(sq, sq_send, sq_recv)
    inverse_row = lax.rsqrt(total_of(sq) / width + EPS)
    inverse = to_columns(inverse_row[0:1], rows, columns)
    pred = state[...] * inverse * gain

    target = tsend[my_rows, :].astype(F32)
    for j in range(1, mn):
        who = (m + j) % mn
        for way in (0, 1):
            for k in range(per):
                place = pl.ds(k * shard + way * half, half)
                pltpu.make_async_remote_copy(
                    src_ref=trecv.at[who, place, :],
                    dst_ref=trecv.at[who, place, :],
                    send_sem=t_send.at[way, k],
                    recv_sem=t_recv.at[who, way, k],
                    device_id={"mp": who},
                    device_id_type=MESH,
                ).wait_recv()
        target = target + trecv[who].astype(F32)

    error = (pred - target) * (tokens ** -0.5)
    err[my_rows, :] = error.astype(BF16)
    errors = Gather(block_of(err), err.at[my_rows, :], mn, m, e_send, e_recv, e_pass)
    errors.start()
    inn[d] = sum_to_row(error * gain * state[...])
    for j in range(1, n):
        exchange(inn, in_send, in_recv, j).start()

    states.finish()
    stores[3].start()

    exchange_wait(inn, in_send, in_recv)
    inner_row = total_of(inn)
    coef[m, 0:8, :] = inverse_row
    coef[m, 8:16, :] = inverse_row * inverse_row * inverse_row * (inner_row / width)

    def coef_copy(j):
        return pltpu.make_async_remote_copy(
            src_ref=coef.at[m], dst_ref=coef.at[m], send_sem=co_send.at[j],
            recv_sem=co_recv.at[m], device_id={"mp": (m + j) % mn}, device_id_type=MESH,
        )

    for j in range(1, mn):
        coef_copy(j).start()
    errors.forward()
    student.finish()
    errors.finish()
    stores[4].start()
    for j in range(1, mn):
        who = (m + j) % mn
        pltpu.make_async_remote_copy(
            src_ref=coef.at[who], dst_ref=coef.at[who], send_sem=co_send.at[j],
            recv_sem=co_recv.at[who], device_id={"mp": who}, device_id_type=MESH,
        ).wait_recv()
    stores[5].start()
    for j in range(1, mn):
        coef_copy(j).wait_send()

    @pl.loop(0, n - 1)
    def _(s):
        for way in (0, 1):
            for k in range(PIECES):
                reduce_copy(s, way, k).wait_send()
                gather_copy(s, way, k).wait_send()

    @pl.loop(0, n)
    def _(owner):
        @pl.when(owner // per != m)
        def _():
            for way in (0, 1):
                target_copy(owner, way).wait_send()

    for one in stores:
        one.wait()


def finish(hid, sall, err, st, coef, gain, grad_wo, grad_gain, grad_proj, grad_state):
    i = pl.program_id(0)
    tokens, columns = err.shape
    rows = coef.shape[2]

    @pl.when(i == 0)
    def _():
        total = jnp.zeros((1, columns), F32)
        for block in range(tokens // rows):
            where = slice(block * rows, (block + 1) * rows)
            wide = err[where, :].astype(F32) * to_columns(coef[block, 0:1], rows, columns)
            kept = st[where, :].astype(F32)
            pull = to_columns(coef[block, 8:9], rows, columns)
            total = total + jnp.sum(wide * kept, axis=0, keepdims=True)
            grad_state[where, :] = (wide * gain[...] - kept * pull).astype(BF16)
        grad_gain[...] = total

    def part(left, right):
        return lax.dot_general(
            left[...], right[...], (((0,), (0,)), ((), ())), preferred_element_type=F32
        )

    grad_proj[...] = -part(hid, err)
    grad_wo[...] = part(sall, grad_state).astype(BF16)


def on_device(
    n,
    mn,
    teacher_query,
    teacher_keys,
    teacher_values,
    teacher_out,
    teacher_resid,
    distill_proj,
    student_context,
    student_resid,
    student_out,
    student_gain,
):
    features, columns = distill_proj.shape
    width = student_context.shape[1]
    rows = teacher_query.shape[0]
    total = rows * mn
    shard = total // n
    vmem = pl.BlockSpec(memory_space=pltpu.VMEM)
    dma = pltpu.SemaphoreType.DMA
    pairs = mn // 2
    gathered = pl.pallas_call(
        functools.partial(middle, n, mn, width, total),
        out_shape=(
            jax.ShapeDtypeStruct((total, features), BF16),
            jax.ShapeDtypeStruct((total, width), BF16),
            jax.ShapeDtypeStruct((total, columns), BF16),
            jax.ShapeDtypeStruct((total, columns), BF16),
            jax.ShapeDtypeStruct((mn, 16, rows), F32),
            jax.ShapeDtypeStruct((1, columns), F32),
        ),
        in_specs=[pl.BlockSpec(memory_space=pltpu.HBM)] * 10,
        out_specs=[pl.BlockSpec(memory_space=pltpu.HBM)] * 6,
        scratch_shapes=[
            pltpu.VMEM((total, features), BF16),
            pltpu.VMEM((total, columns), BF16),
            pltpu.VMEM((total, columns), BF16),
            pltpu.VMEM((mn, 16, rows), F32),
            pltpu.VMEM((1, columns), F32),
            pltpu.VMEM(student_context.shape, BF16),
            pltpu.VMEM(teacher_query.shape, BF16),
            pltpu.VMEM(teacher_resid.shape, BF16),
            pltpu.VMEM(student_resid.shape, BF16),
            pltpu.VMEM((total, 2 * HEAD), BF16),
            pltpu.VMEM((total, teacher_query.shape[1]), BF16),
            pltpu.VMEM(teacher_out.shape, BF16),
            pltpu.VMEM(distill_proj.shape, BF16),
            pltpu.VMEM(student_out.shape, BF16),
            pltpu.VMEM((total, features), BF16),
            pltpu.VMEM((2, n - 1, PIECES, shard // 2, features // PIECES), BF16),
            pltpu.VMEM((total, columns), BF16),
            pltpu.VMEM((mn, rows, columns), BF16),
            pltpu.VMEM((rows, columns), F32),
            pltpu.VMEM((n, 8, rows), F32),
            pltpu.VMEM((n, 8, rows), F32),
            dma((10,)),
            dma((6,)),
            dma((2, n - 1, PIECES)),
            dma((2, n - 1, PIECES)),
            dma((2, n - 1, PIECES)),
            dma((2, n - 1, PIECES)),
            dma((2, n)),
            dma((mn, 2, n // mn)),
            dma((n,)), dma((n,)), dma((n,)), dma((n,)),
            dma((mn,)), dma((mn,)),
            dma((pairs,)), dma((mn,)), dma((pairs,)),
            dma((2, pairs)), dma((2, mn)), dma((2, pairs)),
            dma((pairs,)), dma((mn,)), dma((pairs,)),
            dma((pairs,)), dma((mn,)), dma((pairs,)),
            dma((pairs,)), dma((mn,)), dma((pairs,)),
        ],
        compiler_params=pltpu.CompilerParams(
            collective_id=0, has_side_effects=True, vmem_limit_bytes=VMEM_BYTES
        ),
        name="middle",
    )(
        teacher_query, teacher_keys, teacher_values, teacher_out, teacher_resid, distill_proj,
        student_context, student_resid, student_out, student_gain.reshape(1, width),
    )
    steps = STEPS
    grad_wo, grad_gain, grad_proj = pl.pallas_call(
        finish,
        grid=(steps,),
        out_shape=(
            jax.ShapeDtypeStruct((width, columns), BF16),
            jax.ShapeDtypeStruct((1, columns), F32),
            jax.ShapeDtypeStruct((features, columns), F32),
        ),
        in_specs=[
            pl.BlockSpec((total, features // steps), lambda i: (0, i)),
            pl.BlockSpec((total, width // steps), lambda i: (0, i)),
            vmem, vmem, vmem, vmem,
        ],
        out_specs=(
            pl.BlockSpec((width // steps, columns), lambda i: (i, 0)),
            pl.BlockSpec((1, columns), lambda i: (0, 0)),
            pl.BlockSpec((features // steps, columns), lambda i: (i, 0)),
        ),
        scratch_shapes=[pltpu.VMEM((total, columns), BF16)],
        compiler_params=pltpu.CompilerParams(vmem_limit_bytes=VMEM_BYTES),
        name="finish",
    )(*gathered)
    return (grad_wo, grad_gain.reshape(columns), grad_proj)


def solution(mesh):
    in_specs = (
        P("mp", "dp"),
        P("mp", None),
        P("mp", None),
        P("dp", "mp"),
        P("dp", "mp"),
        P("mp", "dp"),
        P("mp", None),
        P("mp", "dp"),
        P(None, "dp"),
        P(),
    )
    out_specs = (P(None, "dp"), P("dp"), P("mp", "dp"))
    return jax.shard_map(
        functools.partial(on_device, mesh.shape["dp"], mesh.shape["mp"]),
        mesh=mesh, in_specs=in_specs, out_specs=out_specs, check_vma=False,
    )
```

```python
import functools

import jax
import jax.numpy as jnp
from jax import lax
from jax.experimental import pallas as pl
from jax.experimental.pallas import tpu as pltpu
from jax.sharding import PartitionSpec as P

HEADS = 64
KV_HEADS = 8
HEAD = 128
PIECES = 4
PARTS = 4
STEPS = 8
VMEM_BYTES = 56 * 1024 * 1024
EPS = 1e-05
MESH = pl.DeviceIdType.MESH
F32 = jnp.float32
BF16 = jnp.bfloat16


def position_of(index, n):
    z, x = index // 2, index % 2
    return z + x * (n - 1 - 2 * z)


def index_at(position, n):
    side = position // (n // 2)
    return 2 * (position + side * (n - 1 - 2 * position)) + side


class Gather:
    def __init__(self, block, mine, mn, mp, sends, recvs, passes, own=None):
        self.block, self.mine, self.mn, self.mp, self.own = block, mine, mn, mp, own
        self.sends, self.recvs, self.passes = sends, recvs, passes
        self.core, self.group, self.groups = mp % 2, mp // 2, mn // 2
        self.sibling = self.group * 2 + (1 - self.core)

    def same(self, j):
        return ((self.group + j) % self.groups) * 2 + self.core

    def other(self, j):
        return ((self.group + j) % self.groups) * 2 + (1 - self.core)

    def copy(self, source, who, send_sem, target):
        return pltpu.make_async_remote_copy(
            src_ref=source,
            dst_ref=self.block(who),
            send_sem=send_sem,
            recv_sem=self.recvs.at[who],
            device_id={"mp": target},
            device_id_type=MESH,
        )

    def first(self, j):
        target = self.same(j) if j else self.sibling
        return self.copy(self.mine, self.mp, self.sends.at[j], target)

    def start(self):
        for j in range(self.groups):
            self.first(j).start()

    def passed(self, j):
        who = self.same(j)
        return self.copy(self.block(who), who, self.passes.at[j], self.sibling)

    def forward(self):
        for j in range(1, self.groups):
            self.passed(j).wait_recv()
            self.passed(j).start()

    def finish(self):
        for j in range(self.groups):
            who = self.other(j)
            self.copy(self.block(who), who, self.sends.at[j], self.sibling).wait_recv()
        for j in range(self.groups):
            self.first(j).wait_send()
        for j in range(1, self.groups):
            self.passed(j).wait_send()


def to_columns(row, rows, width):
    tile = jnp.transpose(jnp.broadcast_to(row, (128, rows)))
    return jnp.concatenate([tile] * (width // 128), axis=1) if width > 128 else tile


def sum_to_row(values):
    ones = jnp.ones((8, values.shape[1]), F32)
    return lax.dot_general(
        ones, values, (((1,), (1,)), ((), ())),
        precision=lax.Precision.HIGHEST, preferred_element_type=F32,
    )


def middle(
    n, mn, width, tokens,
    query_hbm, keys_hbm, values_hbm, tout_hbm, resid_hbm, proj_hbm, sctx_hbm, sresid_hbm, sout_hbm,
    gain_hbm,
    hid_out, sall, err_out, st_out, coef_out, gain_out,
    hid, err, st, coef, gain_ref, sctx, query, resid, sresid,
    kv, ctx, tout, proj, sout, head, rs, tsend, trecv, state, sq, inn,
    load, store, rs_send, rs_recv, ag_send, ag_recv, t_send, t_recv,
    sq_send, sq_recv, in_send, in_recv, co_send, co_recv,
    k_send, k_recv, k_pass, c_send, c_recv, c_pass,
    s_send, s_recv, s_pass, st_send, st_recv, st_pass, e_send, e_recv, e_pass,
):
    d, m = lax.axis_index("dp"), lax.axis_index("mp")
    rows = tokens // mn
    shard = tokens // n
    half = shard // 2
    per = n // mn
    features, columns = proj.shape
    piece = features // PIECES
    heads = query.shape[1] // HEAD
    p = position_of(d, n)
    my_rows = pl.ds(pl.multiple_of(m * rows, rows), rows)

    kv_cols = pl.ds(pl.multiple_of((d * heads // (HEADS // KV_HEADS)) * HEAD, HEAD), HEAD)
    gain_cols = pl.ds(pl.multiple_of(d * columns, columns), columns)
    loads = [
        pltpu.make_async_copy(src, dst, load.at[i])
        for i, (src, dst) in enumerate(
            (
                (keys_hbm.at[:, kv_cols], kv.at[my_rows, 0:HEAD]),
                (values_hbm.at[:, kv_cols], kv.at[my_rows, HEAD : 2 * HEAD]),
                (sctx_hbm, sctx),
                (sout_hbm, sout),
                (tout_hbm, tout),
                (proj_hbm, proj),
                (query_hbm, query),
                (resid_hbm, resid),
                (sresid_hbm, sresid),
                (gain_hbm.at[:, gain_cols], gain_ref),
            )
        )
    ]
    early = (0, 1, 6)
    for i in early:
        loads[i].start()

    barrier = pltpu.get_barrier_semaphore()
    for j in range(1, n):
        pl.semaphore_signal(barrier, inc=1, device_id={"dp": (d + j) % n}, device_id_type=MESH)
    for j in range(1, mn):
        pl.semaphore_signal(barrier, inc=1, device_id={"mp": (m + j) % mn}, device_id_type=MESH)
    pl.semaphore_wait(barrier, n - 1 + mn - 1)

    def block_of(ref, cols=slice(None)):
        return lambda who: ref.at[pl.ds(pl.multiple_of(who * rows, rows), rows), cols]

    loads[0].wait()
    loads[1].wait()
    pair = Gather(block_of(kv), kv.at[my_rows, :], mn, m, k_send, k_recv, k_pass)
    pair.start()
    for i in (2, 3, 4, 5, 7, 8, 9):
        loads[i].start()

    def exchange(buf, sends, recvs, j):
        return pltpu.make_async_remote_copy(
            src_ref=buf.at[d],
            dst_ref=buf.at[d],
            send_sem=sends.at[j],
            recv_sem=recvs.at[d],
            device_id={"dp": (d + j) % n},
            device_id_type=MESH,
        )

    def exchange_wait(buf, sends, recvs):
        for j in range(1, n):
            who = (d + j) % n
            pltpu.make_async_remote_copy(
                src_ref=buf.at[who], dst_ref=buf.at[who], send_sem=sends.at[j],
                recv_sem=recvs.at[who], device_id={"dp": who}, device_id_type=MESH,
            ).wait_recv()
        for j in range(1, n):
            exchange(buf, sends, recvs, j).wait_send()

    def total_of(buf):
        whole = buf[0]
        for j in range(1, n):
            whole = whole + buf[j]
        return whole

    pair.forward()
    pair.finish()
    loads[6].wait()

    query_pos = m * rows + lax.broadcasted_iota(jnp.int32, (rows, tokens), 0)
    allowed = query_pos >= lax.broadcasted_iota(jnp.int32, (rows, tokens), 1)
    keys, values = kv[:, 0:HEAD], kv[:, HEAD : 2 * HEAD]
    contexts = []
    parts = min(PARTS, heads)
    for part in range(parts):
        for h in range(part * heads // parts, (part + 1) * heads // parts):
            cols = slice(h * HEAD, (h + 1) * HEAD)
            scores = lax.dot_general(
                query[:, cols], keys, (((1,), (1,)), ((), ())), preferred_element_type=F32
            ) * HEAD ** (-0.5)
            scores = jnp.where(allowed, scores, -jnp.inf)
            weights = jnp.exp(scores - jnp.max(scores, axis=1, keepdims=True))
            whole = jnp.sum(weights, axis=1, keepdims=True)
            mixed = jnp.dot(weights.astype(BF16), values, preferred_element_type=F32)
            ctx[my_rows, cols] = (mixed / whole).astype(BF16)
        cols = slice(part * heads // parts * HEAD, (part + 1) * heads // parts * HEAD)
        contexts.append(
            Gather(
                block_of(ctx, cols), ctx.at[my_rows, cols], mn, m,
                c_send.at[part], c_recv.at[part], c_pass.at[part],
            )
        )
        contexts[part].start()
    for part in range(parts - 1):
        contexts[part].forward()
    for i in (2, 3, 8, 9):
        loads[i].wait()
    state[...] = sresid[...].astype(F32) + jnp.dot(sctx[...], sout[...], preferred_element_type=F32)
    contexts[parts - 1].forward()
    st[my_rows, :] = state[...].astype(BF16)
    sq[d] = sum_to_row(state[...] * state[...])
    gain = gain_ref[...]
    for j in range(1, n):
        exchange(sq, sq_send, sq_recv, j).start()
    student = Gather(block_of(sall), sctx, mn, m, s_send, s_recv, s_pass)
    student.start()
    stores = [
        pltpu.make_async_copy(src, dst, store.at[i])
        for i, (src, dst) in enumerate(
            (
                (sctx, sall.at[my_rows, :]),
                (gain_ref, gain_out),
                (hid, hid_out),
                (st, st_out),
                (err, err_out),
                (coef, coef_out),
            )
        )
    ]
    stores[0].start()
    stores[1].start()
    states = Gather(block_of(st), st.at[my_rows, :], mn, m, st_send, st_recv, st_pass)
    states.start()
    loads[4].wait()
    for part in range(parts):
        contexts[part].finish()

    def chunk(position, way):
        start = index_at(position, n) * shard + way * half
        return pl.ds(pl.multiple_of(start, half), half)

    def toward(way):
        return index_at((p + 1 - 2 * way + n) % n, n)

    def at(way, s):
        return (p - (1 - 2 * way) * s + 2 * n) % n

    def cut(k):
        return slice(k * piece, (k + 1) * piece)

    def reduce_copy(s, way, k):
        return pltpu.make_async_remote_copy(
            src_ref=head.at[chunk(at(way, s + 1), way), cut(k)],
            dst_ref=rs.at[way, s, k],
            send_sem=rs_send.at[way, s, k],
            recv_sem=rs_recv.at[way, s, k],
            device_id={"dp": toward(way)},
            device_id_type=MESH,
        )

    for k in range(PIECES):
        head[:, cut(k)] = jnp.dot(
            ctx[...], tout[:, cut(k)], preferred_element_type=F32
        ).astype(BF16)
        for way in (0, 1):
            reduce_copy(0, way, k).start()

    @pl.loop(1, n - 1)
    def _(s):
        for k in range(PIECES):
            for way in (0, 1):
                where = chunk(at(way, s + 1), way)
                reduce_copy(s - 1, way, k).wait_recv()
                summed = head[where, cut(k)].astype(F32) + rs[way, s - 1, k].astype(F32)
                head[where, cut(k)] = summed.astype(BF16)
                reduce_copy(s, way, k).start()

    def moving(s, way, k, where):
        return pltpu.make_async_remote_copy(
            src_ref=hid.at[where, cut(k)],
            dst_ref=hid.at[where, cut(k)],
            send_sem=ag_send.at[way, s, k],
            recv_sem=ag_recv.at[way, s, k],
            device_id={"dp": toward(way)},
            device_id_type=MESH,
        )

    def gather_copy(s, way, k):
        return moving(s, way, k, chunk(at(way, s), way))

    def arrival(s, way, k):
        return moving(s, way, k, chunk(at(way, s + 1), way))

    loads[7].wait()
    for k in range(PIECES):
        for way in (0, 1):
            reduce_copy(n - 2, way, k).wait_recv()
            where = chunk(p, way)
            mine = pl.ds(way * half, half)
            summed = head[where, cut(k)].astype(F32) + rs[way, n - 2, k].astype(F32)
            hid[where, cut(k)] = (resid[mine, cut(k)].astype(F32) + summed).astype(BF16)
            gather_copy(0, way, k).start()

    def target_copy(owner, way):
        to = owner // per
        place = pl.ds(pl.multiple_of((owner % per) * shard + way * half, half), half)
        start = pl.ds(pl.multiple_of(owner * shard + way * half, half), half)
        return pltpu.make_async_remote_copy(
            src_ref=tsend.at[start, :],
            dst_ref=trecv.at[m, place, :],
            send_sem=t_send.at[way, owner],
            recv_sem=t_recv.at[m, way, owner % per],
            device_id={"mp": to},
            device_id_type=MESH,
        )

    def project(s, arrive, forward):
        where = [chunk(at(way, s), way) for way in (0, 1)]
        out = None
        for k in range(PIECES):
            for way in (0, 1):
                if arrive:
                    arrival(s - 1, way, k).wait_recv()
                if forward:
                    gather_copy(s, way, k).start()
            both = jnp.concatenate([hid[w, cut(k)] for w in where], axis=0)
            term = jnp.dot(both, proj[cut(k), :], preferred_element_type=F32)
            out = term if out is None else out + term
        out = out.astype(BF16)
        for way in (0, 1):
            tsend[where[way], :] = out[way * half : (way + 1) * half]
            owner = index_at(at(way, s), n)

            @pl.when(owner // per != m)
            def _():
                target_copy(owner, way).start()

    loads[5].wait()
    project(0, False, False)

    @pl.loop(1, n - 1)
    def _(s):
        project(s, True, True)

    project(n - 1, True, False)
    stores[2].start()
    states.forward()
    student.forward()

    exchange_wait(sq, sq_send, sq_recv)
    inverse_row = lax.rsqrt(total_of(sq) / width + EPS)
    inverse = to_columns(inverse_row[0:1], rows, columns)
    pred = state[...] * inverse * gain

    target = tsend[my_rows, :].astype(F32)
    for j in range(1, mn):
        who = (m + j) % mn
        for way in (0, 1):
            for k in range(per):
                place = pl.ds(k * shard + way * half, half)
                pltpu.make_async_remote_copy(
                    src_ref=trecv.at[who, place, :],
                    dst_ref=trecv.at[who, place, :],
                    send_sem=t_send.at[way, k],
                    recv_sem=t_recv.at[who, way, k],
                    device_id={"mp": who},
                    device_id_type=MESH,
                ).wait_recv()
        target = target + trecv[who].astype(F32)

    error = (pred - target) * (tokens ** -0.5)
    err[my_rows, :] = error.astype(BF16)
    errors = Gather(block_of(err), err.at[my_rows, :], mn, m, e_send, e_recv, e_pass)
    errors.start()
    inn[d] = sum_to_row(error * gain * state[...])
    for j in range(1, n):
        exchange(inn, in_send, in_recv, j).start()

    states.finish()
    stores[3].start()

    exchange_wait(inn, in_send, in_recv)
    inner_row = total_of(inn)
    coef[m, 0:8, :] = inverse_row
    coef[m, 8:16, :] = inverse_row * inverse_row * inverse_row * (inner_row / width)

    def coef_copy(j):
        return pltpu.make_async_remote_copy(
            src_ref=coef.at[m], dst_ref=coef.at[m], send_sem=co_send.at[j],
            recv_sem=co_recv.at[m], device_id={"mp": (m + j) % mn}, device_id_type=MESH,
        )

    for j in range(1, mn):
        coef_copy(j).start()
    errors.forward()
    student.finish()
    errors.finish()
    stores[4].start()
    for j in range(1, mn):
        who = (m + j) % mn
        pltpu.make_async_remote_copy(
            src_ref=coef.at[who], dst_ref=coef.at[who], send_sem=co_send.at[j],
            recv_sem=co_recv.at[who], device_id={"mp": who}, device_id_type=MESH,
        ).wait_recv()
    stores[5].start()
    for j in range(1, mn):
        coef_copy(j).wait_send()

    @pl.loop(0, n - 1)
    def _(s):
        for way in (0, 1):
            for k in range(PIECES):
                reduce_copy(s, way, k).wait_send()
                gather_copy(s, way, k).wait_send()

    @pl.loop(0, n)
    def _(owner):
        @pl.when(owner // per != m)
        def _():
            for way in (0, 1):
                target_copy(owner, way).wait_send()

    for one in stores:
        one.wait()


def finish(hid, sall, err, st, coef, gain, grad_wo, grad_gain, grad_proj, grad_state):
    i = pl.program_id(0)
    tokens, columns = err.shape
    rows = coef.shape[2]

    @pl.when(i == 0)
    def _():
        total = jnp.zeros((1, columns), F32)
        for block in range(tokens // rows):
            where = slice(block * rows, (block + 1) * rows)
            wide = err[where, :].astype(F32) * to_columns(coef[block, 0:1], rows, columns)
            kept = st[where, :].astype(F32)
            pull = to_columns(coef[block, 8:9], rows, columns)
            total = total + jnp.sum(wide * kept, axis=0, keepdims=True)
            grad_state[where, :] = (wide * gain[...] - kept * pull).astype(BF16)
        grad_gain[...] = total

    def part(left, right):
        return lax.dot_general(
            left[...], right[...], (((0,), (0,)), ((), ())), preferred_element_type=F32
        )

    grad_proj[...] = -part(hid, err)
    grad_wo[...] = part(sall, grad_state).astype(BF16)


def on_device(
    n,
    mn,
    teacher_query,
    teacher_keys,
    teacher_values,
    teacher_out,
    teacher_resid,
    distill_proj,
    student_context,
    student_resid,
    student_out,
    student_gain,
):
    features, columns = distill_proj.shape
    width = student_context.shape[1]
    rows = teacher_query.shape[0]
    total = rows * mn
    shard = total // n
    vmem = pl.BlockSpec(memory_space=pltpu.VMEM)
    dma = pltpu.SemaphoreType.DMA
    pairs = mn // 2
    gathered = pl.pallas_call(
        functools.partial(middle, n, mn, width, total),
        out_shape=(
            jax.ShapeDtypeStruct((total, features), BF16),
            jax.ShapeDtypeStruct((total, width), BF16),
            jax.ShapeDtypeStruct((total, columns), BF16),
            jax.ShapeDtypeStruct((total, columns), BF16),
            jax.ShapeDtypeStruct((mn, 16, rows), F32),
            jax.ShapeDtypeStruct((1, columns), F32),
        ),
        in_specs=[pl.BlockSpec(memory_space=pltpu.HBM)] * 10,
        out_specs=[pl.BlockSpec(memory_space=pltpu.HBM)] * 6,
        scratch_shapes=[
            pltpu.VMEM((total, features), BF16),
            pltpu.VMEM((total, columns), BF16),
            pltpu.VMEM((total, columns), BF16),
            pltpu.VMEM((mn, 16, rows), F32),
            pltpu.VMEM((1, columns), F32),
            pltpu.VMEM(student_context.shape, BF16),
            pltpu.VMEM(teacher_query.shape, BF16),
            pltpu.VMEM(teacher_resid.shape, BF16),
            pltpu.VMEM(student_resid.shape, BF16),
            pltpu.VMEM((total, 2 * HEAD), BF16),
            pltpu.VMEM((total, teacher_query.shape[1]), BF16),
            pltpu.VMEM(teacher_out.shape, BF16),
            pltpu.VMEM(distill_proj.shape, BF16),
            pltpu.VMEM(student_out.shape, BF16),
            pltpu.VMEM((total, features), BF16),
            pltpu.VMEM((2, n - 1, PIECES, shard // 2, features // PIECES), BF16),
            pltpu.VMEM((total, columns), BF16),
            pltpu.VMEM((mn, rows, columns), BF16),
            pltpu.VMEM((rows, columns), F32),
            pltpu.VMEM((n, 8, rows), F32),
            pltpu.VMEM((n, 8, rows), F32),
            dma((10,)),
            dma((6,)),
            dma((2, n - 1, PIECES)),
            dma((2, n - 1, PIECES)),
            dma((2, n - 1, PIECES)),
            dma((2, n - 1, PIECES)),
            dma((2, n)),
            dma((mn, 2, n // mn)),
            dma((n,)), dma((n,)), dma((n,)), dma((n,)),
            dma((mn,)), dma((mn,)),
            dma((pairs,)), dma((mn,)), dma((pairs,)),
            dma((PARTS, pairs)), dma((PARTS, mn)), dma((PARTS, pairs)),
            dma((pairs,)), dma((mn,)), dma((pairs,)),
            dma((pairs,)), dma((mn,)), dma((pairs,)),
            dma((pairs,)), dma((mn,)), dma((pairs,)),
        ],
        compiler_params=pltpu.CompilerParams(
            collective_id=0, has_side_effects=True, vmem_limit_bytes=VMEM_BYTES
        ),
        name="middle",
    )(
        teacher_query, teacher_keys, teacher_values, teacher_out, teacher_resid, distill_proj,
        student_context, student_resid, student_out, student_gain.reshape(1, width),
    )
    steps = min(STEPS, features // 128)
    grad_wo, grad_gain, grad_proj = pl.pallas_call(
        finish,
        grid=(steps,),
        out_shape=(
            jax.ShapeDtypeStruct((width, columns), BF16),
            jax.ShapeDtypeStruct((1, columns), F32),
            jax.ShapeDtypeStruct((features, columns), F32),
        ),
        in_specs=[
            pl.BlockSpec((total, features // steps), lambda i: (0, i)),
            pl.BlockSpec((total, width // steps), lambda i: (0, i)),
            vmem, vmem, vmem, vmem,
        ],
        out_specs=(
            pl.BlockSpec((width // steps, columns), lambda i: (i, 0)),
            pl.BlockSpec((1, columns), lambda i: (0, 0)),
            pl.BlockSpec((features // steps, columns), lambda i: (i, 0)),
        ),
        scratch_shapes=[pltpu.VMEM((total, columns), BF16)],
        compiler_params=pltpu.CompilerParams(vmem_limit_bytes=VMEM_BYTES),
        name="finish",
    )(*gathered)
    return (grad_wo, grad_gain.reshape(columns), grad_proj)


def solution(mesh):
    in_specs = (
        P("mp", "dp"),
        P("mp", None),
        P("mp", None),
        P("dp", "mp"),
        P("dp", "mp"),
        P("mp", "dp"),
        P("mp", None),
        P("mp", "dp"),
        P(None, "dp"),
        P(),
    )
    out_specs = (P(None, "dp"), P("dp"), P("mp", "dp"))
    return jax.shard_map(
        functools.partial(on_device, mesh.shape["dp"], mesh.shape["mp"]),
        mesh=mesh, in_specs=in_specs, out_specs=out_specs, check_vma=False,
    )
```

```python
import functools

import jax
import jax.numpy as jnp
from jax import lax
from jax.experimental import pallas as pl
from jax.experimental.pallas import tpu as pltpu
from jax.sharding import PartitionSpec as P

HEADS = 64
KV_HEADS = 8
HEAD = 128
PIECES = 4
PARTS = 4
STEPS = 4
VMEM_BYTES = 56 * 1024 * 1024
EPS = 1e-05
MESH = pl.DeviceIdType.MESH
F32 = jnp.float32
BF16 = jnp.bfloat16


def position_of(index, n):
    z, x = index // 2, index % 2
    return z + x * (n - 1 - 2 * z)


def index_at(position, n):
    side = position // (n // 2)
    return 2 * (position + side * (n - 1 - 2 * position)) + side


class Gather:
    def __init__(self, block, mine, mn, mp, sends, recvs, passes, own=None):
        self.block, self.mine, self.mn, self.mp, self.own = block, mine, mn, mp, own
        self.sends, self.recvs, self.passes = sends, recvs, passes
        self.core, self.group, self.groups = mp % 2, mp // 2, mn // 2
        self.sibling = self.group * 2 + (1 - self.core)

    def same(self, j):
        return ((self.group + j) % self.groups) * 2 + self.core

    def other(self, j):
        return ((self.group + j) % self.groups) * 2 + (1 - self.core)

    def copy(self, source, who, send_sem, target):
        return pltpu.make_async_remote_copy(
            src_ref=source,
            dst_ref=self.block(who),
            send_sem=send_sem,
            recv_sem=self.recvs.at[who],
            device_id={"mp": target},
            device_id_type=MESH,
        )

    def first(self, j):
        target = self.same(j) if j else self.sibling
        return self.copy(self.mine, self.mp, self.sends.at[j], target)

    def start(self):
        for j in range(self.groups):
            self.first(j).start()

    def passed(self, j):
        who = self.same(j)
        return self.copy(self.block(who), who, self.passes.at[j], self.sibling)

    def forward(self):
        for j in range(1, self.groups):
            self.passed(j).wait_recv()
            self.passed(j).start()

    def finish(self):
        for j in range(self.groups):
            who = self.other(j)
            self.copy(self.block(who), who, self.sends.at[j], self.sibling).wait_recv()
        for j in range(self.groups):
            self.first(j).wait_send()
        for j in range(1, self.groups):
            self.passed(j).wait_send()


def to_columns(row, rows, width):
    tile = jnp.transpose(jnp.broadcast_to(row, (128, rows)))
    return jnp.concatenate([tile] * (width // 128), axis=1) if width > 128 else tile


def sum_to_row(values):
    ones = jnp.ones((8, values.shape[1]), F32)
    return lax.dot_general(
        ones, values, (((1,), (1,)), ((), ())),
        precision=lax.Precision.HIGHEST, preferred_element_type=F32,
    )


def middle(
    n, mn, width, tokens,
    query_hbm, keys_hbm, values_hbm, tout_hbm, resid_hbm, proj_hbm, sctx_hbm, sresid_hbm, sout_hbm,
    gain_hbm,
    hid_out, sall, err_out, st_out, coef_out, gain_out,
    hid, err, st, coef, gain_ref, sctx, query, resid, sresid,
    kv, ctx, tout, proj, sout, head, rs, tsend, trecv, state, sq, inn,
    load, store, rs_send, rs_recv, ag_send, ag_recv, t_send, t_recv,
    sq_send, sq_recv, in_send, in_recv, co_send, co_recv,
    k_send, k_recv, k_pass, c_send, c_recv, c_pass,
    s_send, s_recv, s_pass, st_send, st_recv, st_pass, e_send, e_recv, e_pass,
):
    d, m = lax.axis_index("dp"), lax.axis_index("mp")
    rows = tokens // mn
    shard = tokens // n
    half = shard // 2
    per = n // mn
    features, columns = proj.shape
    piece = features // PIECES
    heads = query.shape[1] // HEAD
    p = position_of(d, n)
    my_rows = pl.ds(pl.multiple_of(m * rows, rows), rows)

    kv_cols = pl.ds(pl.multiple_of((d * heads // (HEADS // KV_HEADS)) * HEAD, HEAD), HEAD)
    gain_cols = pl.ds(pl.multiple_of(d * columns, columns), columns)
    loads = [
        pltpu.make_async_copy(src, dst, load.at[i])
        for i, (src, dst) in enumerate(
            (
                (keys_hbm.at[:, kv_cols], kv.at[my_rows, 0:HEAD]),
                (values_hbm.at[:, kv_cols], kv.at[my_rows, HEAD : 2 * HEAD]),
                (sctx_hbm, sctx),
                (sout_hbm, sout),
                (tout_hbm, tout),
                (proj_hbm, proj),
                (query_hbm, query),
                (resid_hbm, resid),
                (sresid_hbm, sresid),
                (gain_hbm.at[:, gain_cols], gain_ref),
            )
        )
    ]
    early = (0, 1, 6)
    for i in early:
        loads[i].start()

    barrier = pltpu.get_barrier_semaphore()
    for j in range(1, n):
        pl.semaphore_signal(barrier, inc=1, device_id={"dp": (d + j) % n}, device_id_type=MESH)
    for j in range(1, mn):
        pl.semaphore_signal(barrier, inc=1, device_id={"mp": (m + j) % mn}, device_id_type=MESH)
    pl.semaphore_wait(barrier, n - 1 + mn - 1)

    def block_of(ref, cols=slice(None)):
        return lambda who: ref.at[pl.ds(pl.multiple_of(who * rows, rows), rows), cols]

    loads[0].wait()
    loads[1].wait()
    pair = Gather(block_of(kv), kv.at[my_rows, :], mn, m, k_send, k_recv, k_pass)
    pair.start()
    for i in (2, 3, 4, 5, 7, 8, 9):
        loads[i].start()

    def exchange(buf, sends, recvs, j):
        return pltpu.make_async_remote_copy(
            src_ref=buf.at[d],
            dst_ref=buf.at[d],
            send_sem=sends.at[j],
            recv_sem=recvs.at[d],
            device_id={"dp": (d + j) % n},
            device_id_type=MESH,
        )

    def exchange_wait(buf, sends, recvs):
        for j in range(1, n):
            who = (d + j) % n
            pltpu.make_async_remote_copy(
                src_ref=buf.at[who], dst_ref=buf.at[who], send_sem=sends.at[j],
                recv_sem=recvs.at[who], device_id={"dp": who}, device_id_type=MESH,
            ).wait_recv()
        for j in range(1, n):
            exchange(buf, sends, recvs, j).wait_send()

    def total_of(buf):
        whole = buf[0]
        for j in range(1, n):
            whole = whole + buf[j]
        return whole

    pair.forward()
    pair.finish()
    loads[6].wait()

    query_pos = m * rows + lax.broadcasted_iota(jnp.int32, (rows, tokens), 0)
    allowed = query_pos >= lax.broadcasted_iota(jnp.int32, (rows, tokens), 1)
    keys, values = kv[:, 0:HEAD], kv[:, HEAD : 2 * HEAD]
    contexts = []
    parts = min(PARTS, heads)
    for part in range(parts):
        for h in range(part * heads // parts, (part + 1) * heads // parts):
            cols = slice(h * HEAD, (h + 1) * HEAD)
            scores = lax.dot_general(
                query[:, cols], keys, (((1,), (1,)), ((), ())), preferred_element_type=F32
            ) * HEAD ** (-0.5)
            scores = jnp.where(allowed, scores, -jnp.inf)
            weights = jnp.exp(scores - jnp.max(scores, axis=1, keepdims=True))
            whole = jnp.sum(weights, axis=1, keepdims=True)
            mixed = jnp.dot(weights.astype(BF16), values, preferred_element_type=F32)
            ctx[my_rows, cols] = (mixed / whole).astype(BF16)
        cols = slice(part * heads // parts * HEAD, (part + 1) * heads // parts * HEAD)
        contexts.append(
            Gather(
                block_of(ctx, cols), ctx.at[my_rows, cols], mn, m,
                c_send.at[part], c_recv.at[part], c_pass.at[part],
            )
        )
        contexts[part].start()
    for part in range(parts - 1):
        contexts[part].forward()
    for i in (2, 3, 8, 9):
        loads[i].wait()
    state[...] = sresid[...].astype(F32) + jnp.dot(sctx[...], sout[...], preferred_element_type=F32)
    contexts[parts - 1].forward()
    st[my_rows, :] = state[...].astype(BF16)
    sq[d] = sum_to_row(state[...] * state[...])
    gain = gain_ref[...]
    for j in range(1, n):
        exchange(sq, sq_send, sq_recv, j).start()
    student = Gather(block_of(sall), sctx, mn, m, s_send, s_recv, s_pass)
    student.start()
    stores = [
        pltpu.make_async_copy(src, dst, store.at[i])
        for i, (src, dst) in enumerate(
            (
                (sctx, sall.at[my_rows, :]),
                (gain_ref, gain_out),
                (hid, hid_out),
                (st, st_out),
                (err, err_out),
                (coef, coef_out),
            )
        )
    ]
    stores[0].start()
    stores[1].start()
    states = Gather(block_of(st), st.at[my_rows, :], mn, m, st_send, st_recv, st_pass)
    states.start()
    loads[4].wait()
    for part in range(parts):
        contexts[part].finish()

    def chunk(position, way):
        start = index_at(position, n) * shard + way * half
        return pl.ds(pl.multiple_of(start, half), half)

    def toward(way):
        return index_at((p + 1 - 2 * way + n) % n, n)

    def at(way, s):
        return (p - (1 - 2 * way) * s + 2 * n) % n

    def cut(k):
        return slice(k * piece, (k + 1) * piece)

    def reduce_copy(s, way, k):
        return pltpu.make_async_remote_copy(
            src_ref=head.at[chunk(at(way, s + 1), way), cut(k)],
            dst_ref=rs.at[way, s, k],
            send_sem=rs_send.at[way, s, k],
            recv_sem=rs_recv.at[way, s, k],
            device_id={"dp": toward(way)},
            device_id_type=MESH,
        )

    for k in range(PIECES):
        head[:, cut(k)] = jnp.dot(
            ctx[...], tout[:, cut(k)], preferred_element_type=F32
        ).astype(BF16)
        for way in (0, 1):
            reduce_copy(0, way, k).start()

    @pl.loop(1, n - 1)
    def _(s):
        for k in range(PIECES):
            for way in (0, 1):
                where = chunk(at(way, s + 1), way)
                reduce_copy(s - 1, way, k).wait_recv()
                summed = head[where, cut(k)].astype(F32) + rs[way, s - 1, k].astype(F32)
                head[where, cut(k)] = summed.astype(BF16)
                reduce_copy(s, way, k).start()

    def moving(s, way, k, where):
        return pltpu.make_async_remote_copy(
            src_ref=hid.at[where, cut(k)],
            dst_ref=hid.at[where, cut(k)],
            send_sem=ag_send.at[way, s, k],
            recv_sem=ag_recv.at[way, s, k],
            device_id={"dp": toward(way)},
            device_id_type=MESH,
        )

    def gather_copy(s, way, k):
        return moving(s, way, k, chunk(at(way, s), way))

    def arrival(s, way, k):
        return moving(s, way, k, chunk(at(way, s + 1), way))

    loads[7].wait()
    for k in range(PIECES):
        for way in (0, 1):
            reduce_copy(n - 2, way, k).wait_recv()
            where = chunk(p, way)
            mine = pl.ds(way * half, half)
            summed = head[where, cut(k)].astype(F32) + rs[way, n - 2, k].astype(F32)
            hid[where, cut(k)] = (resid[mine, cut(k)].astype(F32) + summed).astype(BF16)
            gather_copy(0, way, k).start()

    def target_copy(owner, way):
        to = owner // per
        place = pl.ds(pl.multiple_of((owner % per) * shard + way * half, half), half)
        start = pl.ds(pl.multiple_of(owner * shard + way * half, half), half)
        return pltpu.make_async_remote_copy(
            src_ref=tsend.at[start, :],
            dst_ref=trecv.at[m, place, :],
            send_sem=t_send.at[way, owner],
            recv_sem=t_recv.at[m, way, owner % per],
            device_id={"mp": to},
            device_id_type=MESH,
        )

    def project(s, arrive, forward):
        where = [chunk(at(way, s), way) for way in (0, 1)]
        out = None
        for k in range(PIECES):
            for way in (0, 1):
                if arrive:
                    arrival(s - 1, way, k).wait_recv()
                if forward:
                    gather_copy(s, way, k).start()
            both = jnp.concatenate([hid[w, cut(k)] for w in where], axis=0)
            term = jnp.dot(both, proj[cut(k), :], preferred_element_type=F32)
            out = term if out is None else out + term
        out = out.astype(BF16)
        for way in (0, 1):
            tsend[where[way], :] = out[way * half : (way + 1) * half]
            owner = index_at(at(way, s), n)

            @pl.when(owner // per != m)
            def _():
                target_copy(owner, way).start()

    loads[5].wait()
    project(0, False, False)

    @pl.loop(1, n // 2)
    def _(s):
        project(s, True, True)

    states.forward()
    student.forward()

    @pl.loop(n // 2, n - 1)
    def _(s):
        project(s, True, True)

    project(n - 1, True, False)
    stores[2].start()

    exchange_wait(sq, sq_send, sq_recv)
    inverse_row = lax.rsqrt(total_of(sq) / width + EPS)
    inverse = to_columns(inverse_row[0:1], rows, columns)
    pred = state[...] * inverse * gain

    target = tsend[my_rows, :].astype(F32)
    for j in range(1, mn):
        who = (m + j) % mn
        for way in (0, 1):
            for k in range(per):
                place = pl.ds(k * shard + way * half, half)
                pltpu.make_async_remote_copy(
                    src_ref=trecv.at[who, place, :],
                    dst_ref=trecv.at[who, place, :],
                    send_sem=t_send.at[way, k],
                    recv_sem=t_recv.at[who, way, k],
                    device_id={"mp": who},
                    device_id_type=MESH,
                ).wait_recv()
        target = target + trecv[who].astype(F32)

    error = (pred - target) * (tokens ** -0.5)
    err[my_rows, :] = error.astype(BF16)
    size = rows // 2

    def error_rows(part):
        return lambda who: err.at[pl.ds(pl.multiple_of(who * rows + part * size, size), size), :]

    errors = [
        Gather(
            error_rows(part), error_rows(part)(m), mn, m,
            e_send.at[part], e_recv.at[part], e_pass.at[part],
        )
        for part in (0, 1)
    ]
    for part in (0, 1):
        errors[part].start()
    inn[d] = sum_to_row(error * gain * state[...])
    for j in range(1, n):
        exchange(inn, in_send, in_recv, j).start()

    states.finish()
    stores[3].start()
    for part in (0, 1):
        errors[part].forward()

    exchange_wait(inn, in_send, in_recv)
    inner_row = total_of(inn)
    coef[m, 0:8, :] = inverse_row
    coef[m, 8:16, :] = inverse_row * inverse_row * inverse_row * (inner_row / width)

    def coef_copy(j):
        return pltpu.make_async_remote_copy(
            src_ref=coef.at[m], dst_ref=coef.at[m], send_sem=co_send.at[j],
            recv_sem=co_recv.at[m], device_id={"mp": (m + j) % mn}, device_id_type=MESH,
        )

    for j in range(1, mn):
        coef_copy(j).start()
    student.finish()
    for part in (0, 1):
        errors[part].finish()
    stores[4].start()
    for j in range(1, mn):
        who = (m + j) % mn
        pltpu.make_async_remote_copy(
            src_ref=coef.at[who], dst_ref=coef.at[who], send_sem=co_send.at[j],
            recv_sem=co_recv.at[who], device_id={"mp": who}, device_id_type=MESH,
        ).wait_recv()
    stores[5].start()
    for j in range(1, mn):
        coef_copy(j).wait_send()

    @pl.loop(0, n - 1)
    def _(s):
        for way in (0, 1):
            for k in range(PIECES):
                reduce_copy(s, way, k).wait_send()
                gather_copy(s, way, k).wait_send()

    @pl.loop(0, n)
    def _(owner):
        @pl.when(owner // per != m)
        def _():
            for way in (0, 1):
                target_copy(owner, way).wait_send()

    for one in stores:
        one.wait()


def finish(hid, sall, err, st, coef, gain, grad_wo, grad_gain, grad_proj, grad_state):
    i = pl.program_id(0)
    tokens, columns = err.shape
    rows = coef.shape[2]

    @pl.when(i == 0)
    def _():
        total = jnp.zeros((1, columns), F32)
        for block in range(tokens // rows):
            where = slice(block * rows, (block + 1) * rows)
            wide = err[where, :].astype(F32) * to_columns(coef[block, 0:1], rows, columns)
            kept = st[where, :].astype(F32)
            pull = to_columns(coef[block, 8:9], rows, columns)
            total = total + jnp.sum(wide * kept, axis=0, keepdims=True)
            grad_state[where, :] = (wide * gain[...] - kept * pull).astype(BF16)
        grad_gain[...] = total

    def part(left, right):
        return lax.dot_general(
            left[...], right[...], (((0,), (0,)), ((), ())), preferred_element_type=F32
        )

    grad_proj[...] = -part(hid, err)
    grad_wo[...] = part(sall, grad_state).astype(BF16)


def on_device(
    n,
    mn,
    teacher_query,
    teacher_keys,
    teacher_values,
    teacher_out,
    teacher_resid,
    distill_proj,
    student_context,
    student_resid,
    student_out,
    student_gain,
):
    features, columns = distill_proj.shape
    width = student_context.shape[1]
    rows = teacher_query.shape[0]
    total = rows * mn
    shard = total // n
    vmem = pl.BlockSpec(memory_space=pltpu.VMEM)
    dma = pltpu.SemaphoreType.DMA
    pairs = mn // 2
    gathered = pl.pallas_call(
        functools.partial(middle, n, mn, width, total),
        out_shape=(
            jax.ShapeDtypeStruct((total, features), BF16),
            jax.ShapeDtypeStruct((total, width), BF16),
            jax.ShapeDtypeStruct((total, columns), BF16),
            jax.ShapeDtypeStruct((total, columns), BF16),
            jax.ShapeDtypeStruct((mn, 16, rows), F32),
            jax.ShapeDtypeStruct((1, columns), F32),
        ),
        in_specs=[pl.BlockSpec(memory_space=pltpu.HBM)] * 10,
        out_specs=[pl.BlockSpec(memory_space=pltpu.HBM)] * 6,
        scratch_shapes=[
            pltpu.VMEM((total, features), BF16),
            pltpu.VMEM((total, columns), BF16),
            pltpu.VMEM((total, columns), BF16),
            pltpu.VMEM((mn, 16, rows), F32),
            pltpu.VMEM((1, columns), F32),
            pltpu.VMEM(student_context.shape, BF16),
            pltpu.VMEM(teacher_query.shape, BF16),
            pltpu.VMEM(teacher_resid.shape, BF16),
            pltpu.VMEM(student_resid.shape, BF16),
            pltpu.VMEM((total, 2 * HEAD), BF16),
            pltpu.VMEM((total, teacher_query.shape[1]), BF16),
            pltpu.VMEM(teacher_out.shape, BF16),
            pltpu.VMEM(distill_proj.shape, BF16),
            pltpu.VMEM(student_out.shape, BF16),
            pltpu.VMEM((total, features), BF16),
            pltpu.VMEM((2, n - 1, PIECES, shard // 2, features // PIECES), BF16),
            pltpu.VMEM((total, columns), BF16),
            pltpu.VMEM((mn, rows, columns), BF16),
            pltpu.VMEM((rows, columns), F32),
            pltpu.VMEM((n, 8, rows), F32),
            pltpu.VMEM((n, 8, rows), F32),
            dma((10,)),
            dma((6,)),
            dma((2, n - 1, PIECES)),
            dma((2, n - 1, PIECES)),
            dma((2, n - 1, PIECES)),
            dma((2, n - 1, PIECES)),
            dma((2, n)),
            dma((mn, 2, n // mn)),
            dma((n,)), dma((n,)), dma((n,)), dma((n,)),
            dma((mn,)), dma((mn,)),
            dma((pairs,)), dma((mn,)), dma((pairs,)),
            dma((PARTS, pairs)), dma((PARTS, mn)), dma((PARTS, pairs)),
            dma((pairs,)), dma((mn,)), dma((pairs,)),
            dma((pairs,)), dma((mn,)), dma((pairs,)),
            dma((2, pairs)), dma((2, mn)), dma((2, pairs)),
        ],
        compiler_params=pltpu.CompilerParams(
            collective_id=0, has_side_effects=True, vmem_limit_bytes=VMEM_BYTES
        ),
        name="middle",
    )(
        teacher_query, teacher_keys, teacher_values, teacher_out, teacher_resid, distill_proj,
        student_context, student_resid, student_out, student_gain.reshape(1, width),
    )
    steps = min(STEPS, features // 128)
    grad_wo, grad_gain, grad_proj = pl.pallas_call(
        finish,
        grid=(steps,),
        out_shape=(
            jax.ShapeDtypeStruct((width, columns), BF16),
            jax.ShapeDtypeStruct((1, columns), F32),
            jax.ShapeDtypeStruct((features, columns), F32),
        ),
        in_specs=[
            pl.BlockSpec((total, features // steps), lambda i: (0, i)),
            pl.BlockSpec((total, width // steps), lambda i: (0, i)),
            vmem, vmem, vmem, vmem,
        ],
        out_specs=(
            pl.BlockSpec((width // steps, columns), lambda i: (i, 0)),
            pl.BlockSpec((1, columns), lambda i: (0, 0)),
            pl.BlockSpec((features // steps, columns), lambda i: (i, 0)),
        ),
        scratch_shapes=[pltpu.VMEM((total, columns), BF16)],
        compiler_params=pltpu.CompilerParams(vmem_limit_bytes=VMEM_BYTES),
        name="finish",
    )(*gathered)
    return (grad_wo, grad_gain.reshape(columns), grad_proj)


def solution(mesh):
    in_specs = (
        P("mp", "dp"),
        P("mp", None),
        P("mp", None),
        P("dp", "mp"),
        P("dp", "mp"),
        P("mp", "dp"),
        P("mp", None),
        P("mp", "dp"),
        P(None, "dp"),
        P(),
    )
    out_specs = (P(None, "dp"), P("dp"), P("mp", "dp"))
    return jax.shard_map(
        functools.partial(on_device, mesh.shape["dp"], mesh.shape["mp"]),
        mesh=mesh, in_specs=in_specs, out_specs=out_specs, check_vma=False,
    )
```

```python
import functools

import jax
import jax.numpy as jnp
from jax import lax
from jax.experimental import pallas as pl
from jax.experimental.pallas import tpu as pltpu
from jax.sharding import PartitionSpec as P

HEADS = 64
KV_HEADS = 8
HEAD = 128
PIECES = 2
PARTS = 4
STEPS = 4
VMEM_BYTES = 56 * 1024 * 1024
EPS = 1e-05
MESH = pl.DeviceIdType.MESH
F32 = jnp.float32
BF16 = jnp.bfloat16


def position_of(index, n):
    z, x = index // 2, index % 2
    return z + x * (n - 1 - 2 * z)


def index_at(position, n):
    side = position // (n // 2)
    return 2 * (position + side * (n - 1 - 2 * position)) + side


class Gather:
    def __init__(self, block, mine, mn, mp, sends, recvs, passes, own=None):
        self.block, self.mine, self.mn, self.mp, self.own = block, mine, mn, mp, own
        self.sends, self.recvs, self.passes = sends, recvs, passes
        self.core, self.group, self.groups = mp % 2, mp // 2, mn // 2
        self.sibling = self.group * 2 + (1 - self.core)

    def same(self, j):
        return ((self.group + j) % self.groups) * 2 + self.core

    def other(self, j):
        return ((self.group + j) % self.groups) * 2 + (1 - self.core)

    def copy(self, source, who, send_sem, target):
        return pltpu.make_async_remote_copy(
            src_ref=source,
            dst_ref=self.block(who),
            send_sem=send_sem,
            recv_sem=self.recvs.at[who],
            device_id={"mp": target},
            device_id_type=MESH,
        )

    def first(self, j):
        target = self.same(j) if j else self.sibling
        return self.copy(self.mine, self.mp, self.sends.at[j], target)

    def start(self):
        for j in range(self.groups):
            self.first(j).start()

    def passed(self, j):
        who = self.same(j)
        return self.copy(self.block(who), who, self.passes.at[j], self.sibling)

    def forward(self):
        for j in range(1, self.groups):
            self.passed(j).wait_recv()
            self.passed(j).start()

    def finish(self):
        for j in range(self.groups):
            who = self.other(j)
            self.copy(self.block(who), who, self.sends.at[j], self.sibling).wait_recv()
        for j in range(self.groups):
            self.first(j).wait_send()
        for j in range(1, self.groups):
            self.passed(j).wait_send()


def to_columns(row, rows, width):
    tile = jnp.transpose(jnp.broadcast_to(row, (128, rows)))
    return jnp.concatenate([tile] * (width // 128), axis=1) if width > 128 else tile


def sum_to_row(values):
    ones = jnp.ones((8, values.shape[1]), F32)
    return lax.dot_general(
        ones, values, (((1,), (1,)), ((), ())),
        precision=lax.Precision.HIGHEST, preferred_element_type=F32,
    )


def middle(
    n, mn, width, tokens,
    query_hbm, keys_hbm, values_hbm, tout_hbm, resid_hbm, proj_hbm, sctx_hbm, sresid_hbm, sout_hbm,
    gain_hbm,
    hid_out, sall, err_out, st_out, coef_out, gain_out,
    hid, err, st, coef, gain_ref, sctx, query, resid, sresid,
    kv, ctx, tout, proj, sout, head, rs, tsend, trecv, state, sq, inn,
    load, store, rs_send, rs_recv, ag_send, ag_recv, t_send, t_recv,
    sq_send, sq_recv, in_send, in_recv, co_send, co_recv,
    k_send, k_recv, k_pass, c_send, c_recv, c_pass,
    s_send, s_recv, s_pass, st_send, st_recv, st_pass, e_send, e_recv, e_pass,
):
    d, m = lax.axis_index("dp"), lax.axis_index("mp")
    rows = tokens // mn
    shard = tokens // n
    half = shard // 2
    per = n // mn
    features, columns = proj.shape
    piece = features // PIECES
    heads = query.shape[1] // HEAD
    p = position_of(d, n)
    my_rows = pl.ds(pl.multiple_of(m * rows, rows), rows)

    kv_cols = pl.ds(pl.multiple_of((d * heads // (HEADS // KV_HEADS)) * HEAD, HEAD), HEAD)
    gain_cols = pl.ds(pl.multiple_of(d * columns, columns), columns)
    loads = [
        pltpu.make_async_copy(src, dst, load.at[i])
        for i, (src, dst) in enumerate(
            (
                (keys_hbm.at[:, kv_cols], kv.at[my_rows, 0:HEAD]),
                (values_hbm.at[:, kv_cols], kv.at[my_rows, HEAD : 2 * HEAD]),
                (sctx_hbm, sctx),
                (sout_hbm, sout),
                (tout_hbm, tout),
                (proj_hbm, proj),
                (query_hbm, query),
                (resid_hbm, resid),
                (sresid_hbm, sresid),
                (gain_hbm.at[:, gain_cols], gain_ref),
            )
        )
    ]
    early = (0, 1, 6)
    for i in early:
        loads[i].start()

    barrier = pltpu.get_barrier_semaphore()
    for j in range(1, n):
        pl.semaphore_signal(barrier, inc=1, device_id={"dp": (d + j) % n}, device_id_type=MESH)
    for j in range(1, mn):
        pl.semaphore_signal(barrier, inc=1, device_id={"mp": (m + j) % mn}, device_id_type=MESH)
    pl.semaphore_wait(barrier, n - 1 + mn - 1)

    def block_of(ref, cols=slice(None)):
        return lambda who: ref.at[pl.ds(pl.multiple_of(who * rows, rows), rows), cols]

    loads[0].wait()
    loads[1].wait()
    pair = Gather(block_of(kv), kv.at[my_rows, :], mn, m, k_send, k_recv, k_pass)
    pair.start()
    for i in (2, 3, 4, 5, 7, 8, 9):
        loads[i].start()

    def exchange(buf, sends, recvs, j):
        return pltpu.make_async_remote_copy(
            src_ref=buf.at[d],
            dst_ref=buf.at[d],
            send_sem=sends.at[j],
            recv_sem=recvs.at[d],
            device_id={"dp": (d + j) % n},
            device_id_type=MESH,
        )

    def exchange_wait(buf, sends, recvs):
        for j in range(1, n):
            who = (d + j) % n
            pltpu.make_async_remote_copy(
                src_ref=buf.at[who], dst_ref=buf.at[who], send_sem=sends.at[j],
                recv_sem=recvs.at[who], device_id={"dp": who}, device_id_type=MESH,
            ).wait_recv()
        for j in range(1, n):
            exchange(buf, sends, recvs, j).wait_send()

    def total_of(buf):
        whole = buf[0]
        for j in range(1, n):
            whole = whole + buf[j]
        return whole

    pair.forward()
    pair.finish()
    loads[6].wait()

    query_pos = m * rows + lax.broadcasted_iota(jnp.int32, (rows, tokens), 0)
    allowed = query_pos >= lax.broadcasted_iota(jnp.int32, (rows, tokens), 1)
    keys, values = kv[:, 0:HEAD], kv[:, HEAD : 2 * HEAD]
    contexts = []
    parts = min(PARTS, heads)
    for part in range(parts):
        for h in range(part * heads // parts, (part + 1) * heads // parts):
            cols = slice(h * HEAD, (h + 1) * HEAD)
            scores = lax.dot_general(
                query[:, cols], keys, (((1,), (1,)), ((), ())), preferred_element_type=F32
            ) * HEAD ** (-0.5)
            scores = jnp.where(allowed, scores, -jnp.inf)
            weights = jnp.exp(scores - jnp.max(scores, axis=1, keepdims=True))
            whole = jnp.sum(weights, axis=1, keepdims=True)
            mixed = jnp.dot(weights.astype(BF16), values, preferred_element_type=F32)
            ctx[my_rows, cols] = (mixed / whole).astype(BF16)
        cols = slice(part * heads // parts * HEAD, (part + 1) * heads // parts * HEAD)
        contexts.append(
            Gather(
                block_of(ctx, cols), ctx.at[my_rows, cols], mn, m,
                c_send.at[part], c_recv.at[part], c_pass.at[part],
            )
        )
        contexts[part].start()
    for part in range(parts - 1):
        contexts[part].forward()
    for i in (2, 3, 8, 9):
        loads[i].wait()
    state[...] = sresid[...].astype(F32) + jnp.dot(sctx[...], sout[...], preferred_element_type=F32)
    contexts[parts - 1].forward()
    st[my_rows, :] = state[...].astype(BF16)
    sq[d] = sum_to_row(state[...] * state[...])
    gain = gain_ref[...]
    for j in range(1, n):
        exchange(sq, sq_send, sq_recv, j).start()
    student = Gather(block_of(sall), sctx, mn, m, s_send, s_recv, s_pass)
    student.start()
    stores = [
        pltpu.make_async_copy(src, dst, store.at[i])
        for i, (src, dst) in enumerate(
            (
                (sctx, sall.at[my_rows, :]),
                (gain_ref, gain_out),
                (hid, hid_out),
                (st, st_out),
                (err, err_out),
                (coef, coef_out),
            )
        )
    ]
    stores[0].start()
    stores[1].start()
    states = Gather(block_of(st), st.at[my_rows, :], mn, m, st_send, st_recv, st_pass)
    states.start()
    loads[4].wait()
    for part in range(parts):
        contexts[part].finish()

    def chunk(position, way):
        start = index_at(position, n) * shard + way * half
        return pl.ds(pl.multiple_of(start, half), half)

    def toward(way):
        return index_at((p + 1 - 2 * way + n) % n, n)

    def at(way, s):
        return (p - (1 - 2 * way) * s + 2 * n) % n

    def cut(k):
        return slice(k * piece, (k + 1) * piece)

    def reduce_copy(s, way, k):
        return pltpu.make_async_remote_copy(
            src_ref=head.at[chunk(at(way, s + 1), way), cut(k)],
            dst_ref=rs.at[way, s, k],
            send_sem=rs_send.at[way, s, k],
            recv_sem=rs_recv.at[way, s, k],
            device_id={"dp": toward(way)},
            device_id_type=MESH,
        )

    for k in range(PIECES):
        head[:, cut(k)] = jnp.dot(
            ctx[...], tout[:, cut(k)], preferred_element_type=F32
        ).astype(BF16)
        for way in (0, 1):
            reduce_copy(0, way, k).start()

    @pl.loop(1, n - 1)
    def _(s):
        for k in range(PIECES):
            for way in (0, 1):
                where = chunk(at(way, s + 1), way)
                reduce_copy(s - 1, way, k).wait_recv()
                summed = head[where, cut(k)].astype(F32) + rs[way, s - 1, k].astype(F32)
                head[where, cut(k)] = summed.astype(BF16)
                reduce_copy(s, way, k).start()

    def moving(s, way, k, where):
        return pltpu.make_async_remote_copy(
            src_ref=hid.at[where, cut(k)],
            dst_ref=hid.at[where, cut(k)],
            send_sem=ag_send.at[way, s, k],
            recv_sem=ag_recv.at[way, s, k],
            device_id={"dp": toward(way)},
            device_id_type=MESH,
        )

    def gather_copy(s, way, k):
        return moving(s, way, k, chunk(at(way, s), way))

    def arrival(s, way, k):
        return moving(s, way, k, chunk(at(way, s + 1), way))

    loads[7].wait()
    for k in range(PIECES):
        for way in (0, 1):
            reduce_copy(n - 2, way, k).wait_recv()
            where = chunk(p, way)
            mine = pl.ds(way * half, half)
            summed = head[where, cut(k)].astype(F32) + rs[way, n - 2, k].astype(F32)
            hid[where, cut(k)] = (resid[mine, cut(k)].astype(F32) + summed).astype(BF16)
            gather_copy(0, way, k).start()

    def target_copy(owner, way):
        to = owner // per
        place = pl.ds(pl.multiple_of((owner % per) * shard + way * half, half), half)
        start = pl.ds(pl.multiple_of(owner * shard + way * half, half), half)
        return pltpu.make_async_remote_copy(
            src_ref=tsend.at[start, :],
            dst_ref=trecv.at[m, place, :],
            send_sem=t_send.at[way, owner],
            recv_sem=t_recv.at[m, way, owner % per],
            device_id={"mp": to},
            device_id_type=MESH,
        )

    def project(s, arrive, forward):
        where = [chunk(at(way, s), way) for way in (0, 1)]
        out = None
        for k in range(PIECES):
            for way in (0, 1):
                if arrive:
                    arrival(s - 1, way, k).wait_recv()
                if forward:
                    gather_copy(s, way, k).start()
            both = jnp.concatenate([hid[w, cut(k)] for w in where], axis=0)
            term = jnp.dot(both, proj[cut(k), :], preferred_element_type=F32)
            out = term if out is None else out + term
        out = out.astype(BF16)
        for way in (0, 1):
            tsend[where[way], :] = out[way * half : (way + 1) * half]
            owner = index_at(at(way, s), n)

            @pl.when(owner // per != m)
            def _():
                target_copy(owner, way).start()

    loads[5].wait()
    project(0, False, False)

    @pl.loop(1, n // 2)
    def _(s):
        project(s, True, True)

    states.forward()
    student.forward()

    @pl.loop(n // 2, n - 1)
    def _(s):
        project(s, True, True)

    project(n - 1, True, False)
    stores[2].start()

    exchange_wait(sq, sq_send, sq_recv)
    inverse_row = lax.rsqrt(total_of(sq) / width + EPS)
    inverse = to_columns(inverse_row[0:1], rows, columns)
    pred = state[...] * inverse * gain

    target = tsend[my_rows, :].astype(F32)
    for j in range(1, mn):
        who = (m + j) % mn
        for way in (0, 1):
            for k in range(per):
                place = pl.ds(k * shard + way * half, half)
                pltpu.make_async_remote_copy(
                    src_ref=trecv.at[who, place, :],
                    dst_ref=trecv.at[who, place, :],
                    send_sem=t_send.at[way, k],
                    recv_sem=t_recv.at[who, way, k],
                    device_id={"mp": who},
                    device_id_type=MESH,
                ).wait_recv()
        target = target + trecv[who].astype(F32)

    error = (pred - target) * (tokens ** -0.5)
    err[my_rows, :] = error.astype(BF16)
    size = rows // 2

    def error_rows(part):
        return lambda who: err.at[pl.ds(pl.multiple_of(who * rows + part * size, size), size), :]

    errors = [
        Gather(
            error_rows(part), error_rows(part)(m), mn, m,
            e_send.at[part], e_recv.at[part], e_pass.at[part],
        )
        for part in (0, 1)
    ]
    for part in (0, 1):
        errors[part].start()
    inn[d] = sum_to_row(error * gain * state[...])
    for j in range(1, n):
        exchange(inn, in_send, in_recv, j).start()

    states.finish()
    stores[3].start()
    for part in (0, 1):
        errors[part].forward()

    exchange_wait(inn, in_send, in_recv)
    inner_row = total_of(inn)
    coef[m, 0:8, :] = inverse_row
    coef[m, 8:16, :] = inverse_row * inverse_row * inverse_row * (inner_row / width)

    def coef_copy(j):
        return pltpu.make_async_remote_copy(
            src_ref=coef.at[m], dst_ref=coef.at[m], send_sem=co_send.at[j],
            recv_sem=co_recv.at[m], device_id={"mp": (m + j) % mn}, device_id_type=MESH,
        )

    for j in range(1, mn):
        coef_copy(j).start()
    student.finish()
    for part in (0, 1):
        errors[part].finish()
    stores[4].start()
    for j in range(1, mn):
        who = (m + j) % mn
        pltpu.make_async_remote_copy(
            src_ref=coef.at[who], dst_ref=coef.at[who], send_sem=co_send.at[j],
            recv_sem=co_recv.at[who], device_id={"mp": who}, device_id_type=MESH,
        ).wait_recv()
    stores[5].start()
    for j in range(1, mn):
        coef_copy(j).wait_send()

    @pl.loop(0, n - 1)
    def _(s):
        for way in (0, 1):
            for k in range(PIECES):
                reduce_copy(s, way, k).wait_send()
                gather_copy(s, way, k).wait_send()

    @pl.loop(0, n)
    def _(owner):
        @pl.when(owner // per != m)
        def _():
            for way in (0, 1):
                target_copy(owner, way).wait_send()

    for one in stores:
        one.wait()


def finish(hid, sall, err, st, coef, gain, grad_wo, grad_gain, grad_proj, grad_state):
    i = pl.program_id(0)
    tokens, columns = err.shape
    rows = coef.shape[2]

    @pl.when(i == 0)
    def _():
        total = jnp.zeros((1, columns), F32)
        for block in range(tokens // rows):
            where = slice(block * rows, (block + 1) * rows)
            wide = err[where, :].astype(F32) * to_columns(coef[block, 0:1], rows, columns)
            kept = st[where, :].astype(F32)
            pull = to_columns(coef[block, 8:9], rows, columns)
            total = total + jnp.sum(wide * kept, axis=0, keepdims=True)
            grad_state[where, :] = (wide * gain[...] - kept * pull).astype(BF16)
        grad_gain[...] = total

    def part(left, right):
        return lax.dot_general(
            left[...], right[...], (((0,), (0,)), ((), ())), preferred_element_type=F32
        )

    grad_proj[...] = -part(hid, err)
    grad_wo[...] = part(sall, grad_state).astype(BF16)


def on_device(
    n,
    mn,
    teacher_query,
    teacher_keys,
    teacher_values,
    teacher_out,
    teacher_resid,
    distill_proj,
    student_context,
    student_resid,
    student_out,
    student_gain,
):
    features, columns = distill_proj.shape
    width = student_context.shape[1]
    rows = teacher_query.shape[0]
    total = rows * mn
    shard = total // n
    vmem = pl.BlockSpec(memory_space=pltpu.VMEM)
    dma = pltpu.SemaphoreType.DMA
    pairs = mn // 2
    gathered = pl.pallas_call(
        functools.partial(middle, n, mn, width, total),
        out_shape=(
            jax.ShapeDtypeStruct((total, features), BF16),
            jax.ShapeDtypeStruct((total, width), BF16),
            jax.ShapeDtypeStruct((total, columns), BF16),
            jax.ShapeDtypeStruct((total, columns), BF16),
            jax.ShapeDtypeStruct((mn, 16, rows), F32),
            jax.ShapeDtypeStruct((1, columns), F32),
        ),
        in_specs=[pl.BlockSpec(memory_space=pltpu.HBM)] * 10,
        out_specs=[pl.BlockSpec(memory_space=pltpu.HBM)] * 6,
        scratch_shapes=[
            pltpu.VMEM((total, features), BF16),
            pltpu.VMEM((total, columns), BF16),
            pltpu.VMEM((total, columns), BF16),
            pltpu.VMEM((mn, 16, rows), F32),
            pltpu.VMEM((1, columns), F32),
            pltpu.VMEM(student_context.shape, BF16),
            pltpu.VMEM(teacher_query.shape, BF16),
            pltpu.VMEM(teacher_resid.shape, BF16),
            pltpu.VMEM(student_resid.shape, BF16),
            pltpu.VMEM((total, 2 * HEAD), BF16),
            pltpu.VMEM((total, teacher_query.shape[1]), BF16),
            pltpu.VMEM(teacher_out.shape, BF16),
            pltpu.VMEM(distill_proj.shape, BF16),
            pltpu.VMEM(student_out.shape, BF16),
            pltpu.VMEM((total, features), BF16),
            pltpu.VMEM((2, n - 1, PIECES, shard // 2, features // PIECES), BF16),
            pltpu.VMEM((total, columns), BF16),
            pltpu.VMEM((mn, rows, columns), BF16),
            pltpu.VMEM((rows, columns), F32),
            pltpu.VMEM((n, 8, rows), F32),
            pltpu.VMEM((n, 8, rows), F32),
            dma((10,)),
            dma((6,)),
            dma((2, n - 1, PIECES)),
            dma((2, n - 1, PIECES)),
            dma((2, n - 1, PIECES)),
            dma((2, n - 1, PIECES)),
            dma((2, n)),
            dma((mn, 2, n // mn)),
            dma((n,)), dma((n,)), dma((n,)), dma((n,)),
            dma((mn,)), dma((mn,)),
            dma((pairs,)), dma((mn,)), dma((pairs,)),
            dma((PARTS, pairs)), dma((PARTS, mn)), dma((PARTS, pairs)),
            dma((pairs,)), dma((mn,)), dma((pairs,)),
            dma((pairs,)), dma((mn,)), dma((pairs,)),
            dma((2, pairs)), dma((2, mn)), dma((2, pairs)),
        ],
        compiler_params=pltpu.CompilerParams(
            collective_id=0, has_side_effects=True, vmem_limit_bytes=VMEM_BYTES
        ),
        name="middle",
    )(
        teacher_query, teacher_keys, teacher_values, teacher_out, teacher_resid, distill_proj,
        student_context, student_resid, student_out, student_gain.reshape(1, width),
    )
    steps = min(STEPS, features // 128)
    grad_wo, grad_gain, grad_proj = pl.pallas_call(
        finish,
        grid=(steps,),
        out_shape=(
            jax.ShapeDtypeStruct((width, columns), BF16),
            jax.ShapeDtypeStruct((1, columns), F32),
            jax.ShapeDtypeStruct((features, columns), F32),
        ),
        in_specs=[
            pl.BlockSpec((total, features // steps), lambda i: (0, i)),
            pl.BlockSpec((total, width // steps), lambda i: (0, i)),
            vmem, vmem, vmem, vmem,
        ],
        out_specs=(
            pl.BlockSpec((width // steps, columns), lambda i: (i, 0)),
            pl.BlockSpec((1, columns), lambda i: (0, 0)),
            pl.BlockSpec((features // steps, columns), lambda i: (i, 0)),
        ),
        scratch_shapes=[pltpu.VMEM((total, columns), BF16)],
        compiler_params=pltpu.CompilerParams(vmem_limit_bytes=VMEM_BYTES),
        name="finish",
    )(*gathered)
    return (grad_wo, grad_gain.reshape(columns), grad_proj)


def solution(mesh):
    in_specs = (
        P("mp", "dp"),
        P("mp", None),
        P("mp", None),
        P("dp", "mp"),
        P("dp", "mp"),
        P("mp", "dp"),
        P("mp", None),
        P("mp", "dp"),
        P(None, "dp"),
        P(),
    )
    out_specs = (P(None, "dp"), P("dp"), P("mp", "dp"))
    return jax.shard_map(
        functools.partial(on_device, mesh.shape["dp"], mesh.shape["mp"]),
        mesh=mesh, in_specs=in_specs, out_specs=out_specs, check_vma=False,
    )
```
